512 devices in a mesh: expert: 32 (over z_hi, y), replica: 16 (over x, z_lo, core).
Axes of the slice: x: 4, y: 8, z: 8 (z_hi: 4, z_lo: 2; z = z_hi * 2 + z_lo), core: 2. Of those that a mesh axis runs over, the one named last changes fastest.
Arguments:
- tokens: bfloat16 [16384, 3584], P(('expert', 'replica')), may hold values from -6 to 6
- cotangent: bfloat16 [16384, 3584], P(('expert', 'replica')), may hold values from -6 to 6
- assign: int32 [1024], P(('expert', 'replica')), may hold values from 0 to 3, as said below
- w_gate: bfloat16 [3584, 4096], P(None, 'expert'), may hold values from -0.09375 to 0.09375
- w_up: bfloat16 [3584, 4096], P(None, 'expert'), may hold values from -0.09375 to 0.09375
- w_down: bfloat16 [4096, 3584], P('expert'), may hold values from -0.1875 to 0.1875
Outputs:
- input_grad: bfloat16 [16384, 3584], P(('expert', 'replica'))
- grad_gate: float32 [3584, 4096], P('replica', 'expert')
- grad_up: float32 [3584, 4096], P('replica', 'expert')
- grad_down: float32 [4096, 3584], P('expert', 'replica')
The draws below stay inside these ranges and needn't reach their ends.
Inputs may be any that keep to these rules, and one draw needn't show every extreme that they name: `assign`: block k has replica index (k // 2) % 16. The two blocks 2i and 2i+1 go to two different experts. Let L(e, r) count the blocks of replica index r that go to expert e: for every r one expert has L = 32, every L(e, r) is at least 10, and L(e, r) + L(e, r + 8) is at most 43; both bounds are reached for every r.
All inputs are finite; a program needn't handle non-finite values.
Results may differ from the reference program's by a relative error of at most 0.022.
Values may be sent and summed in bfloat16 or wider, within the bound.
A program may use at most 64 MiB of HBM per device.

```python
import math
import jax
import jax.numpy as jnp
from jax import lax

D = 3584
H = 1024
E_WIN = 4
BLK = 16
ROWS_ALL = 16384
EROWS = 4096
N_EXPERT = 32
N_REPLICA = 16


def draw_assign(key, part):
    key = jax.random.fold_in(key, 11)
    key_low, key_step, key_flip = jax.random.split(key, 3)
    half = N_REPLICA // 2
    low_heavy = jax.random.randint(key_low, (half,), 0, E_WIN)
    step_heavy = jax.random.randint(key_step, (half,), 1, E_WIN)
    high_heavy = (low_heavy + step_heavy) % E_WIN
    heavy = jnp.concatenate([low_heavy, high_heavy])
    partner = jnp.concatenate([high_heavy, low_heavy])
    offset = (partner - heavy - 1) % E_WIN
    source = jnp.arange(N_EXPERT, dtype=jnp.int32)[:, None]
    second = (heavy[None, :] + 1 + (source % 3 + offset[None, :]) % 3) % E_WIN
    first = jnp.broadcast_to(heavy[None, :], (N_EXPERT, N_REPLICA))
    flip = jax.random.randint(key_flip, (N_EXPERT, N_REPLICA), 0, 2)
    block_a = jnp.where(flip == 1, second, first)
    block_b = jnp.where(flip == 1, first, second)
    return jnp.stack([block_a, block_b], axis=-1).reshape(-1).astype(jnp.int32)


def steps_of(rng, shape, pieces, least, largest):
    def one(position, shards_of):
        heights = jax.random.uniform(jax.random.fold_in(jax.random.fold_in(rng, 6), position), (shards_of,), jnp.float32, least / len(pieces), largest / len(pieces))
        return jnp.repeat(jnp.exp(heights), shape[position] // shards_of).reshape((-1,) + (1,) * (len(shape) - position - 1))

    level = one(*pieces[0])
    for cut in pieces[1:]:
        level = level * one(*cut)
    return level


def gaussian(key, dims, scale, bound, pieces=(), kind=jnp.bfloat16):
    values = scale * jax.random.normal(key, dims, jnp.float32)
    if pieces:
        values = values * steps_of(key, dims, pieces, -0.22, 0.18)
    return jnp.clip(values, -bound, bound).astype(kind)


def setup_inputs(seed: int = 0) -> dict:
    seeds = jax.random.split(jax.random.key(seed), 7)
    return {
        "tokens": gaussian(seeds[0], (ROWS_ALL, D), 1.0, 6.0, ((0, 512),)),
        "cotangent": gaussian(seeds[1], (ROWS_ALL, D), 1.0, 6.0, ((0, 512),)),
        "assign": draw_assign(jax.random.fold_in(seeds[6], 71), 0),
        "w_gate": gaussian(seeds[3], (D, E_WIN * H), D ** -0.5, 0.09375, ((1, 32),)),
        "w_up": gaussian(seeds[4], (D, E_WIN * H), D ** -0.5, 0.09375, ((1, 32),)),
        "w_down": gaussian(seeds[5], (E_WIN * H, D), H ** -0.5, 0.1875, ((0, 32),)),
    }


def expert_grads(flat_x, flat_dy, gate_w, up_w, down_w):
    gate_pre = jnp.dot(flat_x, gate_w, preferred_element_type=jnp.float32)
    up_pre = jnp.dot(flat_x, up_w, preferred_element_type=jnp.float32)
    sig_gate = jax.nn.sigmoid(gate_pre)
    silu_gate = gate_pre * sig_gate
    hidden = (silu_gate * up_pre).astype(jnp.bfloat16)
    d_hidden = jnp.dot(flat_dy, down_w.T, preferred_element_type=jnp.float32)
    d_up = (d_hidden * silu_gate).astype(jnp.bfloat16)
    d_gate = (d_hidden * up_pre * sig_gate * (1.0 + gate_pre * (1.0 - sig_gate))).astype(jnp.bfloat16)
    return (hidden, d_gate, d_up)

def settle(value):
    rounded = lax.optimization_barrier(value.astype(jnp.bfloat16))
    return rounded.astype(jnp.float32)

def reference(tokens, cotangent, assign, w_gate, w_up, w_down):
    sharing = N_EXPERT // E_WIN
    shard_width = H // sharing
    row_total = N_EXPERT * BLK
    blocks_x = tokens.reshape(N_EXPERT, N_REPLICA, 2, BLK, D)
    blocks_dy = cotangent.reshape(N_EXPERT, N_REPLICA, 2, BLK, D)
    routes = assign.reshape(N_EXPERT, N_REPLICA, 2)
    zeros_acc = jnp.zeros((E_WIN, D, H), jnp.float32)

    def one_replica(carry, replica_idx):
        acc_gate, acc_up, acc_down = carry
        own_x = lax.dynamic_index_in_dim(blocks_x, replica_idx, 1, keepdims=False)
        own_dy = lax.dynamic_index_in_dim(blocks_dy, replica_idx, 1, keepdims=False)
        own_route = lax.dynamic_index_in_dim(routes, replica_idx, 1, keepdims=False)
        result = jnp.zeros((N_EXPERT, 2, BLK, D), jnp.bfloat16)
        blank_rows = jnp.zeros((N_EXPERT, BLK, D), jnp.bfloat16)
        for expert in range(E_WIN):
            chosen = own_route == expert
            to_first = chosen[:, 0][:, None, None]
            to_second = chosen[:, 1][:, None, None]
            in_x = jnp.where(to_first, own_x[:, 0], jnp.where(to_second, own_x[:, 1], blank_rows)).reshape(row_total, D)
            in_dy = jnp.where(to_first, own_dy[:, 0], jnp.where(to_second, own_dy[:, 1], blank_rows)).reshape(row_total, D)
            gate_w = w_gate[:, expert * H:(expert + 1) * H]
            up_w = w_up[:, expert * H:(expert + 1) * H]
            down_w = w_down[expert * H:(expert + 1) * H, :]
            hidden, d_gate, d_up = expert_grads(in_x, in_dy, gate_w, up_w, down_w)
            gate_f = gate_w.astype(jnp.float32).reshape(D, sharing, shard_width)
            up_f = up_w.astype(jnp.float32).reshape(D, sharing, shard_width)
            gate_d = d_gate.astype(jnp.float32).reshape(row_total, sharing, shard_width)
            up_d = d_up.astype(jnp.float32).reshape(row_total, sharing, shard_width)
            shard_parts = jnp.einsum('rsh,dsh->srd', gate_d, gate_f) + jnp.einsum('rsh,dsh->srd', up_d, up_f)
            summed = lax.optimization_barrier(jnp.sum(settle(shard_parts), axis=0)).astype(jnp.bfloat16).reshape(N_EXPERT, 1, BLK, D)
            result = jnp.where(chosen[:, :, None, None], summed, result)
            part_gate = jnp.dot(in_x.T, d_gate, preferred_element_type=jnp.float32)
            part_up = jnp.dot(in_x.T, d_up, preferred_element_type=jnp.float32)
            part_down = jnp.dot(in_dy.T, hidden, preferred_element_type=jnp.float32)
            acc_gate = acc_gate.at[expert].add(settle(part_gate))
            acc_up = acc_up.at[expert].add(settle(part_up))
            acc_down = acc_down.at[expert].add(settle(part_down))
        return ((acc_gate, acc_up, acc_down), result)
    carry_out, results = lax.scan(one_replica, (zeros_acc, zeros_acc, zeros_acc), jnp.arange(N_REPLICA, dtype=jnp.int32))
    acc_gate, acc_up, acc_down = carry_out
    input_grad = jnp.transpose(results, (1, 0, 2, 3, 4)).reshape(N_EXPERT * N_REPLICA * 2 * BLK, D)
    grad_scale = 1.0 / math.sqrt(EROWS)
    grad_gate = jnp.transpose(acc_gate, (1, 0, 2)).reshape(D, E_WIN * H) * grad_scale
    grad_up = jnp.transpose(acc_up, (1, 0, 2)).reshape(D, E_WIN * H) * grad_scale
    grad_down = jnp.transpose(acc_down, (0, 2, 1)).reshape(E_WIN * H, D) * grad_scale
    return (input_grad, grad_gate, grad_up, grad_down)
```

```python
import functools
import math

import jax
import jax.numpy as jnp
from jax import lax
from jax.experimental import pallas as pl
from jax.experimental.pallas import tpu as pltpu
from jax.sharding import PartitionSpec as P

E_WIN = 4
NY = 8
NX = 4
BLK = 16
D = 3584
SLICE = 128
ROWS = 224
STEP = 512
MESH = pl.DeviceIdType.MESH
LEAN = (1, -1, 1, -1)


def place():
    ex = lax.axis_index("expert")
    rp = lax.axis_index("replica")
    z, y = lax.div(ex, NY), lax.rem(ex, NY)
    q, core = lax.div(rp, 2), lax.rem(rp, 2)
    x, zl = lax.div(q, 2), lax.rem(q, 2)

    def at_z(i):
        return (lax.rem(z + i, E_WIN) * NY + y, rp)

    def at_y(d):
        return (z * NY + lax.rem(y + NY + d, NY), rp)

    def at_x(i):
        return (ex, lax.rem(x + i, NX) * 4 + zl * 2 + core)

    pair = (ex, x * 4 + (1 - zl) * 2 + core)
    sibling = (ex, q * 2 + 1 - core)
    return z, x, zl, q, core, at_z, at_y, at_x, pair, sibling


def greet(peers):
    barrier = pltpu.get_barrier_semaphore()
    for peer in peers:
        pl.semaphore_signal(barrier, inc=1, device_id=peer, device_id_type=MESH)
    pl.semaphore_wait(barrier, len(peers))


def remote(src, dst, send_sem, recv_sem, peer):
    return pltpu.make_async_remote_copy(
        src_ref=src, dst_ref=dst, send_sem=send_sem, recv_sem=recv_sem, device_id=peer, device_id_type=MESH
    )


def dispatch_kernel(send, wg, wu, wd, rows, go, uo, do, zs, zr, ys, yr, ls, ws, wr):
    z, x, zl, q, core, at_z, at_y, at_x, pair, sibling = place()
    greet([at_z(i) for i in (1, 2, 3)] + [at_y(1), at_y(-1), at_y(4)] + [at_x(i) for i in (1, 2, 3)] + [pair, sibling])
    half = pl.ds(pl.multiple_of(core * (D // 2), 128), D // 2)

    def weights(srcs, dsts, base, peer):
        return [remote(s, d, ws.at[base + n], wr.at[base + n], peer) for n, (s, d) in enumerate(zip(srcs, dsts))]

    def start(copies):
        for c in copies:
            c.start()

    one = [go.at[core, q], uo.at[core, q], do.at[q, :, half]]
    stage1 = weights([wg.at[core, q], wu.at[core, q], wd.at[q, :, half]], one, 0, at_y(4))
    stage2 = weights(one, one, 3, pair)
    two = pl.ds(2 * x, 2)
    both = [go.at[core, two], uo.at[core, two], do.at[two, :, half]]
    stage3 = [weights(both, both, 6 + 3 * (i - 1), at_x(i)) for i in (1, 2, 3)]
    every = [go.at[core], uo.at[core], do.at[:, :, half]]
    stage4 = weights(every, every, 15, sibling)

    by_z = {
        4 - i: remote(send.at[lax.rem(z + i, E_WIN)], rows.at[4 - i, 0], zs.at[i - 1], zr.at[3 - i], at_z(i))
        for i in (1, 2, 3)
    }

    def by_y(j):
        src = send.at[z] if j == 0 else rows.at[j, 0]
        s = LEAN[j]
        return [
            remote(src, rows.at[j, 1], ys.at[j, 0], yr.at[j, 0], at_y(s)),
            remote(src, rows.at[j, 2], ys.at[j, 1], yr.at[j, 1], at_y(-s)),
            remote(rows.at[j, 1], rows.at[j, 3], ys.at[j, 2], yr.at[j, 2], at_y(s)),
        ]

    along_y = [by_y(j) for j in range(E_WIN)]
    own = pltpu.make_async_copy(send.at[z], rows.at[0, 0], ls)

    start(stage1)
    for j in (1, 3, 2):
        by_z[j].start()
    start(along_y[0][:2])
    own.start()
    along_y[0][0].wait_recv()
    along_y[0][2].start()
    for c in stage1:
        c.wait_recv()
    start(stage2)
    for j in (1, 3):
        by_z[j].wait_recv()
        start(along_y[j][:2])
    for c in stage2:
        c.wait_recv()
    for group in stage3:
        start(group)
    for j in (1, 3):
        along_y[j][0].wait_recv()
        along_y[j][2].start()
    by_z[2].wait_recv()
    start(along_y[2][:2])
    along_y[2][0].wait_recv()
    along_y[2][2].start()
    for group in stage3:
        for c in group:
            c.wait_recv()
    start(stage4)
    for j in range(E_WIN):
        along_y[j][1].wait_recv()
        along_y[j][2].wait_recv()
    for c in stage4:
        c.wait_recv()
    own.wait()
    for j in (1, 2, 3):
        by_z[j].wait_send()
    for group in along_y + stage3 + [stage1, stage2, stage4]:
        for c in group:
            c.wait_send()


def dispatch(send, wg, wu, wd):
    out = jax.ShapeDtypeStruct
    bf = jnp.bfloat16
    dma = pltpu.SemaphoreType.DMA
    anywhere = pl.BlockSpec(memory_space=pl.ANY)
    rows, go, uo, do = pl.pallas_call(
        dispatch_kernel,
        out_shape=(
            out((E_WIN, 4, BLK, 2 * D), bf),
            out((2, 8, ROWS, SLICE), bf),
            out((2, 8, ROWS, SLICE), bf),
            out((8, BLK, D), bf),
        ),
        in_specs=[anywhere] * 4,
        out_specs=[anywhere] * 4,
        scratch_shapes=[dma((3,)), dma((3,)), dma((4, 3)), dma((4, 3)), dma, dma((18,)), dma((18,))],
        compiler_params=pltpu.CompilerParams(collective_id=0, has_side_effects=True),
        name="dispatch",
    )(send, wg.reshape(2, 8, ROWS, SLICE), wu.reshape(2, 8, ROWS, SLICE), wd.reshape(8, BLK, D))
    return rows.reshape(16 * BLK, 2 * D), go.reshape(D, SLICE), uo.reshape(D, SLICE), do.reshape(SLICE, D)


def expert_kernel(x, dy, wg, go, wu, uo, wd, do, px, dw, pre, dh, dcat, hid):
    phase, step = pl.program_id(0), pl.program_id(1)
    by_cols = (((1,), (1,)), ((), ()))
    by_rows = (((0,), (0,)), ((), ()))
    f32 = jnp.float32

    @pl.when(phase == 0)
    def _():
        @pl.when(step == 0)
        def _():
            pre[...] = jnp.zeros_like(pre)
            dh[...] = jnp.zeros_like(dh)

        w = jnp.concatenate([wg[...], go[...], wu[...], uo[...]], axis=1)
        pre[...] += jnp.dot(x[...], w, preferred_element_type=f32)
        down = jnp.concatenate([wd[...], do[...]], axis=0)
        dh[...] += lax.dot_general(dy[...], down, by_cols, preferred_element_type=f32)

    @pl.when(phase == 1)
    def _():
        @pl.when(step == 0)
        def _():
            gate, up = pre[:, : 2 * SLICE], pre[:, 2 * SLICE :]
            grad = dh[...]
            sig = jax.nn.sigmoid(gate)
            silu = gate * sig
            hid[...] = (silu * up).astype(jnp.bfloat16)
            dcat[:, 2 * SLICE :] = (grad * silu).astype(jnp.bfloat16)
            dcat[:, : 2 * SLICE] = (grad * up * sig * (1.0 + gate * (1.0 - sig))).astype(jnp.bfloat16)

        w = jnp.concatenate([wg[...], go[...], wu[...], uo[...]], axis=1)
        px[...] = lax.dot_general(dcat[...], w, by_cols, preferred_element_type=f32).astype(jnp.bfloat16)
        both = lax.dot_general(x[...], dcat[...], by_rows, preferred_element_type=f32).astype(jnp.bfloat16)
        dw[0] = both[:, : 2 * SLICE]
        dw[1] = both[:, 2 * SLICE :]
        dw[2] = lax.dot_general(dy[...], hid[...], by_rows, preferred_element_type=f32).astype(jnp.bfloat16)


def expert(rows, wg, go, wu, uo, wd, do):
    n = rows.shape[0]
    steps = D // STEP
    bf = jnp.bfloat16
    tall = pl.BlockSpec((STEP, SLICE), lambda p, k: (k, 0))
    wide = pl.BlockSpec((SLICE, STEP), lambda p, k: (0, k))
    return pl.pallas_call(
        expert_kernel,
        grid=(2, steps),
        out_shape=(jax.ShapeDtypeStruct((n, D), bf), jax.ShapeDtypeStruct((3, D, 2 * SLICE), bf)),
        in_specs=[
            pl.BlockSpec((n, STEP), lambda p, k: (0, k)),
            pl.BlockSpec((n, STEP), lambda p, k: (0, k + steps)),
            tall, tall, tall, tall, wide, wide,
        ],
        out_specs=(
            pl.BlockSpec((n, STEP), lambda p, k: (0, k * p)),
            pl.BlockSpec((3, STEP, 2 * SLICE), lambda p, k: (0, k * p, 0)),
        ),
        scratch_shapes=[
            pltpu.VMEM((n, 4 * SLICE), jnp.float32),
            pltpu.VMEM((n, 2 * SLICE), jnp.float32),
            pltpu.VMEM((n, 4 * SLICE), bf),
            pltpu.VMEM((n, 2 * SLICE), bf),
        ],
        compiler_params=pltpu.CompilerParams(vmem_limit_bytes=40 * 2**20),
        cost_estimate=pl.CostEstimate(flops=16 * n * D * 2 * SLICE, bytes_accessed=30 * 2**20, transcendentals=0),
        name="expert",
    )(rows, rows, wg, go, wu, uo, wd, do)


def combine_kernel(scale, px, dw, ret, out, parts, sums, mine, theirs, from_x, s2, from_z, s3, from_y,
                   ls, ps, pr, zs, zr, c_s, c_r, xs, xr, gs, gr, ys, yr):
    z, x, zl, q, core, at_z, at_y, at_x, pair, sibling = place()
    f32, bf = jnp.float32, jnp.bfloat16
    greet([at_z(i) for i in (1, 2, 3)] + [at_y(d) for d in (1, -1, 2, -2, 4)] + [at_x(i) for i in (1, 2, 3)] + [pair, sibling])

    to_core = [remote(dw.at[k, :, 1 - core], theirs.at[k], c_s.at[k], c_r.at[k], sibling) for k in range(3)]
    keep = [pltpu.make_async_copy(dw.at[k, :, core], mine.at[k], ls.at[k]) for k in range(3)]
    own = [pltpu.make_async_copy(px.at[j, 0], parts.at[j, 0], ls.at[3 + j]) for j in range(E_WIN)]
    back = [
        [
            remote(px.at[j, o], parts.at[j, o], ps.at[j, o - 1], pr.at[j, o - 1], at_y(d * LEAN[j]))
            for o, d in ((1, -1), (2, 1), (3, -2))
        ]
        for j in range(E_WIN)
    ]
    to_x = [
        [
            remote(mine.at[k, pl.ds(2 * lax.rem(x + i, NX), 2)], from_x.at[k, i - 1], xs.at[k, i - 1], xr.at[k, i - 1], at_x(i))
            for i in (1, 2, 3)
        ]
        for k in range(3)
    ]
    to_pair = [remote(s2.at[k, 1 - zl], from_z.at[k], gs.at[k], gr.at[k], pair) for k in range(3)]
    to_y = [remote(s3.at[k, 1], from_y.at[k], ys.at[k], yr.at[k], at_y(4)) for k in range(3)]
    home = {j: remote(sums.at[j], ret.at[z], zs.at[j - 1], zr.at[j - 1], at_z(j)) for j in (1, 2, 3)}
    stay = pltpu.make_async_copy(sums.at[0], ret.at[z], ls.at[7])
    landing = {j: remote(sums.at[j], ret.at[lax.rem(z + 4 - j, E_WIN)], zs.at[j - 1], zr.at[j - 1], at_z(j)) for j in (1, 2, 3)}

    to_core[0].start()
    keep[0].start()
    for k in (1, 2):
        to_core[k].start()
        keep[k].start()
    for j in (2, 1, 3, 0):
        own[j].start()
        for c in back[j]:
            c.start()

    for k in range(3):
        keep[k].wait()
        to_core[k].wait_recv()

        @pl.loop(0, 8)
        def _(n):
            mine[k, n] = (mine[k, n].astype(f32) + theirs[k, n].astype(f32)).astype(bf)

        for c in to_x[k]:
            c.start()

    for j in (2, 1, 3, 0):
        own[j].wait()
        for c in back[j]:
            c.wait_recv()
        total = parts[j, 0].astype(f32)
        for o in (1, 2, 3):
            total += parts[j, o].astype(f32)
        sums[j] = total.astype(bf)
        if j:
            home[j].start()
        else:
            stay.start()

    for k in range(3):
        for c in to_x[k]:
            c.wait_recv()
        for n in range(2):
            total = mine[k, 2 * x + n].astype(f32)
            for i in range(3):
                total += from_x[k, i, n].astype(f32)
            s2[k, n] = total.astype(bf)
        to_pair[k].start()

    for k in range(3):
        to_pair[k].wait_recv()
        total = s2[k, zl].astype(f32) + from_z[k].astype(f32)
        s3[k, 0] = total[:, :SLICE].astype(bf)
        s3[k, 1] = total[:, SLICE:].astype(bf)
        to_y[k].start()

    for k in range(3):
        to_y[k].wait_recv()
        out[k] = (s3[k, 0].astype(f32) + from_y[k].astype(f32)) * scale

    stay.wait()
    for j in (1, 2, 3):
        landing[j].wait_recv()
        home[j].wait_send()
    for group in back + to_x + [to_core, to_pair, to_y]:
        for c in group:
            c.wait_send()


def combine(px, dw, scale):
    bf = jnp.bfloat16
    dma = pltpu.SemaphoreType.DMA
    anywhere = pl.BlockSpec(memory_space=pl.ANY)
    return pl.pallas_call(
        functools.partial(combine_kernel, scale),
        out_shape=(
            jax.ShapeDtypeStruct((E_WIN, BLK, D), bf),
            jax.ShapeDtypeStruct((3, ROWS, SLICE), jnp.float32),
        ),
        in_specs=[anywhere] * 2,
        out_specs=(anywhere, pl.BlockSpec(memory_space=pltpu.VMEM)),
        scratch_shapes=[
            pltpu.VMEM((E_WIN, 4, BLK, D), bf),
            pltpu.VMEM((E_WIN, BLK, D), bf),
            pltpu.VMEM((3, 8, ROWS, 2 * SLICE), bf),
            pltpu.VMEM((3, 8, ROWS, 2 * SLICE), bf),
            pltpu.VMEM((3, 3, 2, ROWS, 2 * SLICE), bf),
            pltpu.VMEM((3, 2, ROWS, 2 * SLICE), bf),
            pltpu.VMEM((3, ROWS, 2 * SLICE), bf),
            pltpu.VMEM((3, 2, ROWS, SLICE), bf),
            pltpu.VMEM((3, ROWS, SLICE), bf),
            dma((8,)),
            dma((4, 3)), dma((4, 3)),
            dma((3,)), dma((3,)),
            dma((3,)), dma((3,)),
            dma((3, 3)), dma((3, 3)),
            dma((3,)), dma((3,)),
            dma((3,)), dma((3,)),
        ],
        compiler_params=pltpu.CompilerParams(collective_id=1, has_side_effects=True, vmem_limit_bytes=40 * 2**20),
        name="combine",
    )(px.reshape(E_WIN, 4, BLK, D), dw.reshape(3, 8, 2, ROWS, 2 * SLICE))


def shards(tokens, cotangent, assign, w_gate, w_up, w_down):
    scale = 1.0 / math.sqrt(lax.axis_size("expert") * lax.axis_size("replica") * BLK // 2)
    own = jnp.concatenate([tokens, cotangent], axis=1).reshape(2, BLK, 2 * D)
    experts = jnp.arange(E_WIN, dtype=jnp.int32)
    first = (assign[0] == experts)[:, None, None]
    second = (assign[1] == experts)[:, None, None]
    send = jnp.where(first, own[0], jnp.where(second, own[1], jnp.zeros((), jnp.bfloat16)))
    rows, go, uo, do = dispatch(send, w_gate, w_up, w_down)
    px, dw = expert(rows, w_gate, go, w_up, uo, w_down, do)
    ret, grads = combine(px, dw, scale)
    picked = jnp.zeros((2, BLK, D), jnp.bfloat16)
    for e in range(E_WIN):
        picked = jnp.where((assign == e)[:, None, None], ret[e], picked)
    return picked.reshape(2 * BLK, D), grads[0], grads[1], jnp.transpose(grads[2])


def solution(mesh):
    placed = (
        P(("expert", "replica"), None),
        P(("expert", "replica"), None),
        P(("expert", "replica")),
        P(None, "expert"),
        P(None, "expert"),
        P("expert", None),
    )
    return jax.shard_map(
        shards,
        mesh=mesh,
        in_specs=placed,
        out_specs=(
            P(("expert", "replica"), None),
            P("replica", "expert"),
            P("replica", "expert"),
            P("expert", "replica"),
        ),
        check_vma=False,
    )
```

```python
import functools
import math

import jax
import jax.numpy as jnp
from jax import lax
from jax.experimental import pallas as pl
from jax.experimental.pallas import tpu as pltpu
from jax.sharding import PartitionSpec as P

E_WIN = 4
NY = 8
NX = 4
BLK = 16
D = 3584
SLICE = 128
ROWS = 224
CHUNK = 896
N_ROWS = 256
MESH = pl.DeviceIdType.MESH
LEAN = (1, -1, 1, -1)
ORDER = (0, 1, 3, 2)


def place():
    ex = lax.axis_index("expert")
    rp = lax.axis_index("replica")
    z, y = lax.div(ex, NY), lax.rem(ex, NY)
    q, core = lax.div(rp, 2), lax.rem(rp, 2)
    x, zl = lax.div(q, 2), lax.rem(q, 2)

    def at_z(i):
        return (lax.rem(z + i, E_WIN) * NY + y, rp)

    def at_y(d):
        return (z * NY + lax.rem(y + NY + d, NY), rp)

    def at_x(i):
        return (ex, lax.rem(x + NX + i, NX) * 4 + zl * 2 + core)

    pair = (ex, x * 4 + (1 - zl) * 2 + core)
    sibling = (ex, q * 2 + 1 - core)
    return z, x, zl, q, core, at_z, at_y, at_x, pair, sibling


def remote(src, dst, send_sem, recv_sem, peer):
    return pltpu.make_async_remote_copy(
        src_ref=src, dst_ref=dst, send_sem=send_sem, recv_sem=recv_sem, device_id=peer, device_id_type=MESH
    )


def start(copies):
    for c in copies:
        c.start()


def slot(j, o):
    return pl.ds((ORDER.index(j) * 4 + o) * BLK, BLK)


def layer_kernel(scale, assign, tokens, cotangent, wg, wu, wd, ret, out,
                 send, rows, w, down, pre, dh, dcat, hid, px, dw, theirs, from_a, from_b, s2, from_z, s3, from_y, parts, sums,
                 ls, zs, zr, ys, yr, ws, wr, ps, pr, hs, hr, cs, cr, as_, ar, bs, br, gs, gr, fs, fr):
    f32, bf = jnp.float32, jnp.bfloat16
    by_cols = (((1,), (1,)), ((), ()))
    by_rows = (((0,), (0,)), ((), ()))
    z, x, zl, q, core, at_z, at_y, at_x, pair, sibling = place()

    peers = [at_z(i) for i in (1, 2, 3)] + [at_y(d) for d in (1, -1, 2, -2, 4)] + [at_x(i) for i in (1, 2, 3)] + [pair, sibling]
    barrier = pltpu.get_barrier_semaphore()
    for peer in peers:
        pl.semaphore_signal(barrier, inc=1, device_id=peer, device_id_type=MESH)

    keep = [
        pltpu.make_async_copy(wg, w.at[:, 0:SLICE], ls.at[0]),
        pltpu.make_async_copy(wu, w.at[:, 2 * SLICE : 3 * SLICE], ls.at[1]),
        pltpu.make_async_copy(wd, down.at[0:SLICE], ls.at[2]),
    ]
    start(keep)
    for c, src in enumerate((tokens, cotangent)):
        first, second = src[0:BLK], src[BLK : 2 * BLK]
        for e in range(E_WIN):
            other = jnp.where(assign[1] == e, second, jnp.zeros_like(second))
            send[c, e] = jnp.where(assign[0] == e, first, other)
        rows[c, slot(0, 0)] = send[c, z]
    pl.semaphore_wait(barrier, len(peers))

    half = pl.ds(pl.multiple_of(core * (D // 2), 128), D // 2)

    def weights(srcs, dsts, base, peer):
        return [remote(s, d, ws.at[base + n], wr.at[base + n], peer) for n, (s, d) in enumerate(zip(srcs, dsts))]

    def part(first, count):
        tall = pl.ds(pl.multiple_of(core * (D // 2) + first * ROWS, 32), count * ROWS)
        short = pl.ds(pl.multiple_of(SLICE + first * BLK, 16), count * BLK)
        return [w.at[tall, SLICE : 2 * SLICE], w.at[tall, 3 * SLICE : 4 * SLICE], down.at[short, half]]

    tall = pl.ds(pl.multiple_of(core * (D // 2) + q * ROWS, 32), ROWS)
    short = pl.ds(pl.multiple_of(q * BLK, 16), BLK)
    one, two, every = part(q, 1), part(2 * x, 2), part(0, 8)
    stage1 = weights([wg.at[tall], wu.at[tall], wd.at[short, half]], one, 0, at_y(4))
    stage2 = weights(one, one, 3, pair)
    stage3 = [weights(two, two, 6 + 3 * (i - 1), at_x(i)) for i in (1, 2, 3)]
    stage4 = weights(every, every, 15, sibling)

    by_z = {
        4 - i: [
            remote(send.at[c, lax.rem(z + i, E_WIN)], rows.at[c, slot(4 - i, 0)], zs.at[i - 1, c], zr.at[3 - i, c], at_z(i))
            for c in (0, 1)
        ]
        for i in (1, 2, 3)
    }

    def by_y(j, c):
        s = LEAN[j]
        return [
            remote(rows.at[c, slot(j, 0)], rows.at[c, slot(j, 1)], ys.at[j, 0, c], yr.at[j, 0, c], at_y(s)),
            remote(rows.at[c, slot(j, 0)], rows.at[c, slot(j, 2)], ys.at[j, 1, c], yr.at[j, 1, c], at_y(-s)),
            remote(rows.at[c, slot(j, 1)], rows.at[c, slot(j, 3)], ys.at[j, 2, c], yr.at[j, 2, c], at_y(s)),
        ]

    along_y = [[by_y(j, c) for c in (0, 1)] for j in range(E_WIN)]

    def spread(j):
        for c in (0, 1):
            if j:
                by_z[j][c].wait_recv()
            start(along_y[j][c][:2])

    def relay(j):
        for c in (0, 1):
            along_y[j][c][0].wait_recv()
            along_y[j][c][2].start()

    def landed(j):
        for c in (0, 1):
            along_y[j][c][1].wait_recv()
            along_y[j][c][2].wait_recv()

    def forward(lo, hi):
        pre[lo:hi] = jnp.zeros((hi - lo, 4 * SLICE), f32)
        dh[lo:hi] = jnp.zeros((hi - lo, 2 * SLICE), f32)

        @pl.loop(0, D // CHUNK)
        def _(n):
            cols = pl.ds(pl.multiple_of(n * CHUNK, 128), CHUNK)
            pre[lo:hi] += jnp.dot(rows[0, lo:hi, cols], w[cols, :], preferred_element_type=f32)
            dh[lo:hi] += lax.dot_general(rows[1, lo:hi, cols], down[:, cols], by_cols, preferred_element_type=f32)

    start(stage1)
    for c in (0, 1):
        by_z[3][c].start()
        by_z[1][c].start()
    spread(0)
    relay(0)
    start(by_z[2])
    for c in stage1:
        c.wait_recv()
    start(stage2)
    spread(1)
    spread(3)
    for c in stage2:
        c.wait_recv()
    for group in stage3:
        start(group)
    relay(1)
    relay(3)
    spread(2)
    for group in stage3:
        for c in group:
            c.wait_recv()
    start(stage4)
    relay(2)
    for c in keep:
        c.wait()
    for c in stage4:
        c.wait_recv()
    for j in ORDER[:3]:
        landed(j)
    forward(0, 3 * 64)
    landed(2)
    forward(3 * 64, N_ROWS)

    gate, up, grad = pre[:, : 2 * SLICE], pre[:, 2 * SLICE :], dh[...]
    sig = jax.nn.sigmoid(gate)
    silu = gate * sig
    hid[...] = (silu * up).astype(bf)
    dcat[:, 2 * SLICE :] = (grad * silu).astype(bf)
    dcat[:, : 2 * SLICE] = (grad * up * sig * (1.0 + gate * (1.0 - sig))).astype(bf)

    to_core = [remote(dw.at[k, :, 1 - core], theirs.at[k], cs.at[k], cr.at[k], sibling) for k in range(3)]
    ahead, beyond, behind = lax.rem(x + 1, NX), lax.rem(x + 2, NX), lax.rem(x + 3, NX)

    def grad_rows(k, target, n):
        return dw.at[k, 2 * target + n, core]

    by_a = [
        [
            remote(grad_rows(k, beyond, 0), from_a.at[k, 0], as_.at[k, 0], ar.at[k, 0], at_x(1)),
            remote(grad_rows(k, beyond, 1), from_a.at[k, 1], as_.at[k, 1], ar.at[k, 1], at_x(-1)),
        ]
        for k in range(3)
    ]
    by_b = [
        [
            remote(grad_rows(k, ahead, 1), from_b.at[k, 0, 1], bs.at[k, 0], br.at[k, 0], at_x(1)),
            remote(grad_rows(k, behind, 0), from_b.at[k, 1, 0], bs.at[k, 1], br.at[k, 1], at_x(-1)),
            remote(grad_rows(k, ahead, 0), from_b.at[k, 0, 0], bs.at[k, 2], br.at[k, 2], at_x(1)),
            remote(grad_rows(k, behind, 1), from_b.at[k, 1, 1], bs.at[k, 3], br.at[k, 3], at_x(-1)),
        ]
        for k in range(3)
    ]
    to_pair = [remote(s2.at[k, 1 - zl], from_z.at[k], gs.at[k], gr.at[k], pair) for k in range(3)]
    to_y = [remote(s3.at[k, 1], from_y.at[k], fs.at[k], fr.at[k], at_y(4)) for k in range(3)]

    def weight_grad(k):
        left = rows.at[k // 2]

        @pl.loop(0, D // CHUNK)
        def _(n):
            cols = pl.ds(pl.multiple_of(n * CHUNK, 128), CHUNK)
            right = hid[...] if k == 2 else dcat[:, 2 * SLICE * k : 2 * SLICE * (k + 1)]
            full = lax.dot_general(left[:, cols], right, by_rows, preferred_element_type=f32)
            dw[k, pl.ds(2 * n, 2)] = full.astype(bf).reshape(2, 2, ROWS, 2 * SLICE)

        to_core[k].start()

    def over_cores(k):
        to_core[k].wait_recv()

        @pl.loop(0, 8)
        def _(n):
            dw[k, n, core] = (dw[k, n, core].astype(f32) + theirs[k, n].astype(f32)).astype(bf)

        start(by_a[k])
        start(by_b[k][:2])

    def augment(k):
        for c, (target, n) in zip(by_a[k], ((ahead, 0), (behind, 1))):
            c.wait_recv()
            place_ = grad_rows(k, target, n)
            place_[...] = (place_[...].astype(f32) + from_a[k, n].astype(f32)).astype(bf)
        start(by_b[k][2:])

    def over_x(k):
        for c in by_b[k]:
            c.wait_recv()
        for n in (0, 1):
            total = dw[k, 2 * x + n, core].astype(f32) + from_b[k, 0, n].astype(f32) + from_b[k, 1, n].astype(f32)
            s2[k, n] = total.astype(bf)
        to_pair[k].start()

    def over_pair(k):
        to_pair[k].wait_recv()
        total = s2[k, zl].astype(f32) + from_z[k].astype(f32)
        s3[k, 0] = total[:, :SLICE].astype(bf)
        s3[k, 1] = total[:, SLICE:].astype(bf)
        to_y[k].start()

    def over_y(k):
        to_y[k].wait_recv()
        out[k] = (s3[k, 0].astype(f32) + from_y[k].astype(f32)) * scale

    back = [
        [
            remote(px.at[slot(j, o)], parts.at[j, o - 1], ps.at[j, o - 1], pr.at[j, o - 1], at_y(d * LEAN[j]))
            for o, d in ((1, -1), (2, 1), (3, -2))
        ]
        for j in range(E_WIN)
    ]
    home = {j: remote(sums.at[j], ret.at[z], hs.at[j - 1], hr.at[j - 1], at_z(j)) for j in (1, 2, 3)}
    landing = {j: remote(sums.at[j], ret.at[lax.rem(z + 4 - j, E_WIN)], hs.at[j - 1], hr.at[j - 1], at_z(j)) for j in (1, 2, 3)}
    stay = pltpu.make_async_copy(sums.at[0], ret.at[z], ls.at[3])

    def input_grad():
        @pl.loop(0, D // CHUNK)
        def _(n):
            cols = pl.ds(pl.multiple_of(n * CHUNK, 128), CHUNK)
            px[:, cols] = lax.dot_general(dcat[...], w[cols, :], by_cols, preferred_element_type=f32).astype(bf)

        for j in (2, 1, 3, 0):
            start(back[j][::-1])

    def gather(j):
        for c in back[j]:
            c.wait_recv()
        total = px[slot(j, 0)].astype(f32)
        for o in range(3):
            total += parts[j, o].astype(f32)
        sums[j] = total.astype(bf)
        if j:
            home[j].start()
        else:
            stay.start()

    weight_grad(0)
    input_grad()
    weight_grad(1)
    over_cores(0)
    weight_grad(2)
    over_cores(1)
    over_cores(2)
    augment(0)
    gather(2)
    augment(1)
    gather(1)
    augment(2)
    over_x(0)
    gather(3)
    over_pair(0)
    over_x(1)
    gather(0)
    over_pair(1)
    over_y(0)
    over_x(2)
    over_pair(2)
    over_y(1)
    over_y(2)

    stay.wait()
    for j in (1, 2, 3):
        landing[j].wait_recv()
        home[j].wait_send()
    groups = list(by_z.values()) + [g for both in along_y for g in both] + stage3 + [stage1, stage2, stage4]
    for group in groups + back + by_a + by_b + [to_core, to_pair, to_y]:
        for c in group:
            c.wait_send()


def layer(assign, tokens, cotangent, wg, wu, wd, scale):
    f32, bf = jnp.float32, jnp.bfloat16
    dma = pltpu.SemaphoreType.DMA
    anywhere = pl.BlockSpec(memory_space=pl.ANY)
    vmem = pl.BlockSpec(memory_space=pltpu.VMEM)
    return pl.pallas_call(
        functools.partial(layer_kernel, scale),
        out_shape=(
            jax.ShapeDtypeStruct((E_WIN, BLK, D), bf),
            jax.ShapeDtypeStruct((3, ROWS, SLICE), f32),
        ),
        in_specs=[pl.BlockSpec(memory_space=pltpu.SMEM), vmem, vmem, anywhere, anywhere, anywhere],
        out_specs=(anywhere, vmem),
        scratch_shapes=[
            pltpu.VMEM((2, E_WIN, BLK, D), bf),
            pltpu.VMEM((2, N_ROWS, D), bf),
            pltpu.VMEM((D, 4 * SLICE), bf),
            pltpu.VMEM((2 * SLICE, D), bf),
            pltpu.VMEM((N_ROWS, 4 * SLICE), f32),
            pltpu.VMEM((N_ROWS, 2 * SLICE), f32),
            pltpu.VMEM((N_ROWS, 4 * SLICE), bf),
            pltpu.VMEM((N_ROWS, 2 * SLICE), bf),
            pltpu.VMEM((N_ROWS, D), bf),
            pltpu.VMEM((3, 8, 2, ROWS, 2 * SLICE), bf),
            pltpu.VMEM((3, 8, ROWS, 2 * SLICE), bf),
            pltpu.VMEM((3, 2, ROWS, 2 * SLICE), bf),
            pltpu.VMEM((3, 2, 2, ROWS, 2 * SLICE), bf),
            pltpu.VMEM((3, 2, ROWS, 2 * SLICE), bf),
            pltpu.VMEM((3, ROWS, 2 * SLICE), bf),
            pltpu.VMEM((3, 2, ROWS, SLICE), bf),
            pltpu.VMEM((3, ROWS, SLICE), bf),
            pltpu.VMEM((E_WIN, 3, BLK, D), bf),
            pltpu.VMEM((E_WIN, BLK, D), bf),
            dma((4,)),
            dma((3, 2)), dma((3, 2)),
            dma((4, 3, 2)), dma((4, 3, 2)),
            dma((18,)), dma((18,)),
            dma((4, 3)), dma((4, 3)),
            dma((3,)), dma((3,)),
            dma((3,)), dma((3,)),
            dma((3, 2)), dma((3, 2)),
            dma((3, 4)), dma((3, 4)),
            dma((3,)), dma((3,)),
            dma((3,)), dma((3,)),
        ],
        compiler_params=pltpu.CompilerParams(collective_id=0, has_side_effects=True, vmem_limit_bytes=56 * 2**20),
        cost_estimate=pl.CostEstimate(flops=16 * N_ROWS * D * 2 * SLICE, bytes_accessed=2**24, transcendentals=0),
        name="layer",
    )(assign, tokens, cotangent, wg, wu, wd)


def shards(tokens, cotangent, assign, w_gate, w_up, w_down):
    scale = 1.0 / math.sqrt(lax.axis_size("expert") * lax.axis_size("replica") * BLK // 2)
    ret, grads = layer(assign, tokens, cotangent, w_gate, w_up, w_down, scale)
    picked = jnp.zeros((2, BLK, D), jnp.bfloat16)
    for e in range(E_WIN):
        picked = jnp.where((assign == e)[:, None, None], ret[e], picked)
    return picked.reshape(2 * BLK, D), grads[0], grads[1], jnp.transpose(grads[2])


def solution(mesh):
    placed = (
        P(("expert", "replica"), None),
        P(("expert", "replica"), None),
        P(("expert", "replica")),
        P(None, "expert"),
        P(None, "expert"),
        P("expert", None),
    )
    return jax.shard_map(
        shards,
        mesh=mesh,
        in_specs=placed,
        out_specs=(
            P(("expert", "replica"), None),
            P("replica", "expert"),
            P("replica", "expert"),
            P("expert", "replica"),
        ),
        check_vma=False,
    )
```

```python
import functools
import math

import jax
import jax.numpy as jnp
from jax import lax
from jax.experimental import pallas as pl
from jax.experimental.pallas import tpu as pltpu
from jax.sharding import PartitionSpec as P

E_WIN = 4
NY = 8
NX = 4
BLK = 16
D = 3584
SLICE = 128
ROWS = 224
CHUNK = 896
N_ROWS = 256
MESH = pl.DeviceIdType.MESH
LEAN = (1, -1, 1, -1)
ORDER = (0, 1, 3, 2)


def place():
    ex = lax.axis_index("expert")
    rp = lax.axis_index("replica")
    z, y = lax.div(ex, NY), lax.rem(ex, NY)
    q, core = lax.div(rp, 2), lax.rem(rp, 2)
    x, zl = lax.div(q, 2), lax.rem(q, 2)

    def at_z(i):
        return (lax.rem(z + i, E_WIN) * NY + y, rp)

    def at_y(d):
        return (z * NY + lax.rem(y + NY + d, NY), rp)

    def at_x(i):
        return (ex, lax.rem(x + NX + i, NX) * 4 + zl * 2 + core)

    pair = (ex, x * 4 + (1 - zl) * 2 + core)
    sibling = (ex, q * 2 + 1 - core)
    return z, x, zl, q, core, at_z, at_y, at_x, pair, sibling


def remote(src, dst, send_sem, recv_sem, peer):
    return pltpu.make_async_remote_copy(
        src_ref=src, dst_ref=dst, send_sem=send_sem, recv_sem=recv_sem, device_id=peer, device_id_type=MESH
    )


def start(copies):
    for c in copies:
        c.start()


def slot(j, o):
    return pl.ds((ORDER.index(j) * 4 + o) * BLK, BLK)


def layer_kernel(scale, assign, tokens, cotangent, wg, wu, wd, grad_in, out_gate, out_up, out_down,
                 own, send, rows, w, down, pre, dh, dcat, hid, px, dw, theirs, from_pair, from_a, from_b, s2, from_z, s3, from_y,
                 parts, sums, ret,
                 ls, zs, zr, ys, yr, ws, wr, ps, pr, hs, hr, cs, cr, as_, ar, bs, br, gs, gr, fs, fr):
    f32, bf = jnp.float32, jnp.bfloat16
    by_cols = (((1,), (1,)), ((), ()))
    by_rows = (((0,), (0,)), ((), ()))
    z, x, zl, q, core, at_z, at_y, at_x, pair, sibling = place()

    peers = [at_z(i) for i in (1, 2, 3)] + [at_y(d) for d in (1, -1, 2, -2, 4)] + [at_x(i) for i in (1, 2, 3)] + [pair, sibling]
    barrier = pltpu.get_barrier_semaphore()
    for peer in peers:
        pl.semaphore_signal(barrier, inc=1, device_id=peer, device_id_type=MESH)

    bring = [pltpu.make_async_copy(src, own.at[c], ls.at[3 + c]) for c, src in enumerate((tokens, cotangent))]
    start(bring)
    keep = [
        pltpu.make_async_copy(wg, w.at[:, 0:SLICE], ls.at[0]),
        pltpu.make_async_copy(wu, w.at[:, SLICE : 2 * SLICE], ls.at[1]),
        pltpu.make_async_copy(wd, down.at[0:SLICE], ls.at[2]),
    ]
    for c in (0, 1):
        bring[c].wait()
        first, second = own[c, 0:BLK], own[c, BLK : 2 * BLK]
        for e in range(E_WIN):
            other = jnp.where(assign[1] == e, second, jnp.zeros_like(second))
            send[c, e] = jnp.where(assign[0] == e, first, other)
        rows[c, slot(0, 0)] = send[c, z]
    pl.semaphore_wait(barrier, len(peers))

    half = pl.ds(pl.multiple_of(core * (D // 2), 128), D // 2)

    def weights(srcs, dsts, base, peer):
        return [remote(s, d, ws.at[base + n], wr.at[base + n], peer) for n, (s, d) in enumerate(zip(srcs, dsts))]

    def part(first, count):
        tall = pl.ds(pl.multiple_of(core * (D // 2) + first * ROWS, 32), count * ROWS)
        short = pl.ds(pl.multiple_of(SLICE + first * BLK, 16), count * BLK)
        return [w.at[tall, 2 * SLICE : 3 * SLICE], w.at[tall, 3 * SLICE : 4 * SLICE], down.at[short, half]]

    tall = pl.ds(pl.multiple_of(core * (D // 2) + q * ROWS, 32), ROWS)
    short = pl.ds(pl.multiple_of(q * BLK, 16), BLK)
    one, two, every = part(q, 1), part(2 * x, 2), part(0, 8)
    stage1 = weights([wg.at[tall], wu.at[tall], wd.at[short, half]], one, 0, at_y(4))
    stage2 = weights(one, one, 3, pair)
    stage3 = [weights(two, two, 6 + 3 * (i - 1), at_x(i)) for i in (1, 2, 3)]
    stage4 = weights(every, every, 15, sibling)

    by_z = {
        4 - i: [
            remote(send.at[c, lax.rem(z + i, E_WIN)], rows.at[c, slot(4 - i, 0)], zs.at[i - 1, c], zr.at[3 - i, c], at_z(i))
            for c in (0, 1)
        ]
        for i in (1, 2, 3)
    }

    def by_y(j, c):
        s = LEAN[j]
        return [
            remote(rows.at[c, slot(j, 0)], rows.at[c, slot(j, 1)], ys.at[j, 0, c], yr.at[j, 0, c], at_y(s)),
            remote(rows.at[c, slot(j, 0)], rows.at[c, slot(j, 2)], ys.at[j, 1, c], yr.at[j, 1, c], at_y(-s)),
            remote(rows.at[c, slot(j, 1)], rows.at[c, slot(j, 3)], ys.at[j, 2, c], yr.at[j, 2, c], at_y(s)),
        ]

    along_y = [[by_y(j, c) for c in (0, 1)] for j in range(E_WIN)]

    def spread(j, c):
        if j:
            by_z[j][c].wait_recv()
        start(along_y[j][c][:2])

    def relay(j, c):
        along_y[j][c][0].wait_recv()
        along_y[j][c][2].start()

    def landed(j):
        for c in (0, 1):
            along_y[j][c][1].wait_recv()
            along_y[j][c][2].wait_recv()

    def arrived(stage):
        for c in stage:
            c.wait_recv()

    def forward(lo, hi):
        pre[lo:hi] = jnp.zeros((hi - lo, 4 * SLICE), f32)
        dh[lo:hi] = jnp.zeros((hi - lo, 2 * SLICE), f32)

        @pl.loop(0, D // CHUNK)
        def _(n):
            cols = pl.ds(pl.multiple_of(n * CHUNK, 128), CHUNK)
            pre[lo:hi] += jnp.dot(rows[0, lo:hi, cols], w[cols, :], preferred_element_type=f32)
            dh[lo:hi] += lax.dot_general(rows[1, lo:hi, cols], down[:, cols], by_cols, preferred_element_type=f32)

    start(stage1)
    for c in (0, 1):
        by_z[3][c].start()
        by_z[1][c].start()
        spread(0, c)
    start(keep)
    relay(0, 0)
    start(by_z[2])
    spread(1, 0)
    spread(3, 0)
    relay(0, 1)
    spread(1, 1)
    spread(3, 1)
    arrived(stage1)
    start(stage2)
    relay(1, 0)
    relay(3, 0)
    arrived(stage2)
    for group in stage3:
        start(group)
    relay(1, 1)
    relay(3, 1)
    spread(2, 0)
    spread(2, 1)
    relay(2, 0)
    relay(2, 1)
    for group in stage3:
        arrived(group)
    start(stage4)
    for c in keep:
        c.wait()
    arrived(stage4)
    for j in ORDER[:3]:
        landed(j)
    forward(0, 3 * 64)
    landed(2)
    forward(3 * 64, N_ROWS)

    for h in (0, 1):
        a, b, c = 2 * h * SLICE, (2 * h + 1) * SLICE, (2 * h + 2) * SLICE
        gate, up, grad = pre[:, a:b], pre[:, b:c], dh[:, h * SLICE : (h + 1) * SLICE]
        sig = jax.nn.sigmoid(gate)
        silu = gate * sig
        hid[:, h * SLICE : (h + 1) * SLICE] = (silu * up).astype(bf)
        dcat[:, b:c] = (grad * silu).astype(bf)
        dcat[:, a:b] = (grad * up * sig * (1.0 + gate * (1.0 - sig))).astype(bf)

    near = {off: lax.rem(x + off, NX) for off in range(NX)}
    NEAR = (2, 1, 3, 0)
    LOW = ROWS // 2

    to_core = [
        {off: remote(dw.at[k, n, :, 1 - core], theirs.at[k, n], cs.at[k, off], cr.at[k, off], sibling) for off, n in near.items()}
        for k in range(3)
    ]
    first_pair = {off: remote(dw.at[0, n, 1 - zl, core], from_pair.at[n], gs.at[off], gr.at[off], pair) for off, n in near.items()}

    def piece(k, off, t):
        n = near[off]
        return dw.at[k, n, t, core] if k else dw.at[0, n, zl, core, LOW * t : LOW * (t + 1)]

    def in_a(k, t):
        return from_a.at[k, t] if k else from_a.at[0, t, 0:LOW]

    def in_b(k, side, t):
        return from_b.at[k, side, t] if k else from_b.at[0, side, t, 0:LOW]

    by_a = [
        [
            remote(piece(k, 2, 0), in_a(k, 0), as_.at[k, 0], ar.at[k, 0], at_x(1)),
            remote(piece(k, 2, 1), in_a(k, 1), as_.at[k, 1], ar.at[k, 1], at_x(-1)),
        ]
        for k in range(3)
    ]
    by_b = [
        [
            remote(piece(k, 1, 1), in_b(k, 0, 1), bs.at[k, 0], br.at[k, 0], at_x(1)),
            remote(piece(k, 3, 0), in_b(k, 1, 0), bs.at[k, 1], br.at[k, 1], at_x(-1)),
            remote(piece(k, 1, 0), in_b(k, 0, 0), bs.at[k, 2], br.at[k, 2], at_x(1)),
            remote(piece(k, 3, 1), in_b(k, 1, 1), bs.at[k, 3], br.at[k, 3], at_x(-1)),
        ]
        for k in range(3)
    ]
    to_pair = {k: remote(s2.at[k - 1, 1 - zl], from_z.at[k - 1], gs.at[3 + k], gr.at[3 + k], pair) for k in (1, 2)}
    to_y = {
        1: remote(s3.at[0], from_y.at[0:2], fs.at[0], fr.at[0], at_y(4)),
        2: remote(s3.at[1, 1], from_y.at[2], fs.at[1], fr.at[1], at_y(4)),
    }

    def weight_grad(k):
        for off in NEAR:
            n = near[off]
            cols = pl.ds(pl.multiple_of(n * CHUNK, 128), CHUNK)
            right = hid[...] if k == 2 else dcat[:, 2 * SLICE * k : 2 * SLICE * (k + 1)]
            full = lax.dot_general(rows[k // 2, :, cols], right, by_rows, preferred_element_type=f32)
            dw[k, n] = full.astype(bf).reshape(2, 2, ROWS, 2 * SLICE)
            to_core[k][off].start()

    def leave_x(k, off):
        if off == 2:
            start(by_a[k])
        elif off:
            by_b[k][off // 2].start()

    def over_cores(k):
        for off in NEAR:
            n = near[off]
            to_core[k][off].wait_recv()
            for t in (0, 1):
                dw[k, n, t, core] = (dw[k, n, t, core].astype(f32) + theirs[k, n, t].astype(f32)).astype(bf)
            if k:
                leave_x(k, off)
            else:
                first_pair[off].start()

    def over_pair_first():
        for off in NEAR:
            n = near[off]
            first_pair[off].wait_recv()
            dw[0, n, zl, core] = (dw[0, n, zl, core].astype(f32) + from_pair[n].astype(f32)).astype(bf)
            leave_x(0, off)

    def augment(k):
        for t, off in ((0, 1), (1, 3)):
            by_a[k][t].wait_recv()
            spot = piece(k, off, t)
            spot[...] = (spot[...].astype(f32) + in_a(k, t)[...].astype(f32)).astype(bf)
            by_b[k][2 + t].start()

    def x_total(k, t):
        return piece(k, 0, t)[...].astype(f32) + in_b(k, 0, t)[...].astype(f32) + in_b(k, 1, t)[...].astype(f32)

    def over_x(k):
        for c in by_b[k]:
            c.wait_recv()
        if k:
            s2[k - 1, 1 - zl] = x_total(k, 1 - zl).astype(bf)
            to_pair[k].start()
            s2[k - 1, zl] = x_total(k, zl).astype(bf)
        else:
            for t in (0, 1):
                total = x_total(0, t) * scale
                out_gate[LOW * t : LOW * (t + 1)] = total[:, :SLICE]
                out_up[LOW * t : LOW * (t + 1)] = total[:, SLICE:]

    def over_pair(k):
        to_pair[k].wait_recv()
        total = s2[k - 1, zl].astype(f32) + from_z[k - 1].astype(f32)
        s3[k - 1, 0] = total[:, :SLICE].astype(bf)
        s3[k - 1, 1] = total[:, SLICE:].astype(bf)
        to_y[k].start()

    def over_y(k):
        to_y[k].wait_recv()
        if k == 1:
            out_gate[...] += from_y[0].astype(f32) * scale
            out_up[...] += from_y[1].astype(f32) * scale
        else:
            out_down[...] = (s3[1, 0].astype(f32) + from_y[2].astype(f32)) * scale

    back = [
        [
            remote(px.at[slot(j, o)], parts.at[j, o - 1], ps.at[j, o - 1], pr.at[j, o - 1], at_y(d * LEAN[j]))
            for o, d in ((1, -1), (2, 1), (3, -2))
        ]
        for j in range(E_WIN)
    ]
    home = {j: remote(sums.at[j], ret.at[z], hs.at[j - 1], hr.at[j - 1], at_z(j)) for j in (1, 2, 3)}
    landing = {j: remote(sums.at[j], ret.at[lax.rem(z + 4 - j, E_WIN)], hs.at[j - 1], hr.at[j - 1], at_z(j)) for j in (1, 2, 3)}

    def input_grad():
        @pl.loop(0, D // CHUNK)
        def _(n):
            cols = pl.ds(pl.multiple_of(n * CHUNK, 128), CHUNK)
            px[:, cols] = lax.dot_general(dcat[...], w[cols, :], by_cols, preferred_element_type=f32).astype(bf)

        for j in (2, 1, 3, 0):
            start(back[j][::-1])

    def gather(j):
        arrived(back[j])
        total = px[slot(j, 0)].astype(f32)
        for o in range(3):
            total += parts[j, o].astype(f32)
        if j:
            sums[j] = total.astype(bf)
            home[j].start()
        else:
            ret[z] = total.astype(bf)

    weight_grad(1)
    weight_grad(0)
    over_cores(1)
    input_grad()
    over_cores(0)
    weight_grad(2)
    augment(1)
    over_cores(2)
    over_x(1)
    augment(2)
    over_pair_first()
    over_pair(1)
    augment(0)
    gather(2)
    over_x(2)
    gather(1)
    gather(3)
    over_pair(2)
    gather(0)
    over_x(0)
    over_y(1)
    over_y(2)

    for j in (1, 2, 3):
        landing[j].wait_recv()
    for b in (0, 1):
        mine = ret[0]
        for e in range(1, E_WIN):
            mine = jnp.where(assign[b] == e, ret[e], mine)
        grad_in[b * BLK : (b + 1) * BLK] = mine

    groups = list(by_z.values()) + [g for both in along_y for g in both] + stage3 + [stage1, stage2, stage4]
    groups += back + by_a + by_b + [list(g.values()) for g in to_core + [first_pair, to_pair, to_y, home]]
    for group in groups:
        for c in group:
            c.wait_send()


def layer(assign, tokens, cotangent, wg, wu, wd, scale):
    f32, bf = jnp.float32, jnp.bfloat16
    dma = pltpu.SemaphoreType.DMA
    anywhere = pl.BlockSpec(memory_space=pl.ANY)
    vmem = pl.BlockSpec(memory_space=pltpu.VMEM)
    return pl.pallas_call(
        functools.partial(layer_kernel, scale),
        out_shape=(
            jax.ShapeDtypeStruct((2 * BLK, D), bf),
            jax.ShapeDtypeStruct((ROWS, SLICE), f32),
            jax.ShapeDtypeStruct((ROWS, SLICE), f32),
            jax.ShapeDtypeStruct((ROWS, SLICE), f32),
        ),
        in_specs=[pl.BlockSpec(memory_space=pltpu.SMEM)] + [anywhere] * 5,
        out_specs=(vmem, vmem, vmem, vmem),
        scratch_shapes=[
            pltpu.VMEM((2, 2 * BLK, D), bf),
            pltpu.VMEM((2, E_WIN, BLK, D), bf),
            pltpu.VMEM((2, N_ROWS, D), bf),
            pltpu.VMEM((D, 4 * SLICE), bf),
            pltpu.VMEM((2 * SLICE, D), bf),
            pltpu.VMEM((N_ROWS, 4 * SLICE), f32),
            pltpu.VMEM((N_ROWS, 2 * SLICE), f32),
            pltpu.VMEM((N_ROWS, 4 * SLICE), bf),
            pltpu.VMEM((N_ROWS, 2 * SLICE), bf),
            pltpu.VMEM((N_ROWS, D), bf),
            pltpu.VMEM((3, NX, 2, 2, ROWS, 2 * SLICE), bf),
            pltpu.VMEM((3, NX, 2, ROWS, 2 * SLICE), bf),
            pltpu.VMEM((NX, ROWS, 2 * SLICE), bf),
            pltpu.VMEM((3, 2, ROWS, 2 * SLICE), bf),
            pltpu.VMEM((3, 2, 2, ROWS, 2 * SLICE), bf),
            pltpu.VMEM((2, 2, ROWS, 2 * SLICE), bf),
            pltpu.VMEM((2, ROWS, 2 * SLICE), bf),
            pltpu.VMEM((2, 2, ROWS, SLICE), bf),
            pltpu.VMEM((3, ROWS, SLICE), bf),
            pltpu.VMEM((E_WIN, 3, BLK, D), bf),
            pltpu.VMEM((E_WIN, BLK, D), bf),
            pltpu.VMEM((E_WIN, BLK, D), bf),
            dma((5,)),
            dma((3, 2)), dma((3, 2)),
            dma((4, 3, 2)), dma((4, 3, 2)),
            dma((18,)), dma((18,)),
            dma((4, 3)), dma((4, 3)),
            dma((3,)), dma((3,)),
            dma((3, 4)), dma((3, 4)),
            dma((3, 2)), dma((3, 2)),
            dma((3, 4)), dma((3, 4)),
            dma((6,)), dma((6,)),
            dma((2,)), dma((2,)),
        ],
        compiler_params=pltpu.CompilerParams(collective_id=0, has_side_effects=True, vmem_limit_bytes=56 * 2**20),
        cost_estimate=pl.CostEstimate(flops=16 * N_ROWS * D * 2 * SLICE, bytes_accessed=2**24, transcendentals=0),
        name="layer",
    )(assign, tokens, cotangent, wg, wu, wd)


def shards(tokens, cotangent, assign, w_gate, w_up, w_down):
    scale = 1.0 / math.sqrt(lax.axis_size("expert") * lax.axis_size("replica") * BLK // 2)
    grad_in, gate, up, down = layer(assign, tokens, cotangent, w_gate, w_up, w_down, scale)
    return grad_in, gate, up, jnp.transpose(down)


def solution(mesh):
    placed = (
        P(("expert", "replica"), None),
        P(("expert", "replica"), None),
        P(("expert", "replica")),
        P(None, "expert"),
        P(None, "expert"),
        P("expert", None),
    )
    return jax.shard_map(
        shards,
        mesh=mesh,
        in_specs=placed,
        out_specs=(
            P(("expert", "replica"), None),
            P("replica", "expert"),
            P("replica", "expert"),
            P("expert", "replica"),
        ),
        check_vma=False,
    )
```

```python
import functools
import math

import jax
import jax.numpy as jnp
from jax import lax
from jax.experimental import pallas as pl
from jax.experimental.pallas import tpu as pltpu
from jax.sharding import PartitionSpec as P

E_WIN = 4
NY = 8
NX = 4
BLK = 16
D = 3584
SLICE = 128
ROWS = 224
CHUNK = 896
N_ROWS = 256
MESH = pl.DeviceIdType.MESH
LEAN = (1, -1, 1, -1)
ORDER = (0, 1, 3, 2)


def place():
    ex = lax.axis_index("expert")
    rp = lax.axis_index("replica")
    z, y = lax.div(ex, NY), lax.rem(ex, NY)
    q, core = lax.div(rp, 2), lax.rem(rp, 2)
    x, zl = lax.div(q, 2), lax.rem(q, 2)

    def at_z(i):
        return (lax.rem(z + i, E_WIN) * NY + y, rp)

    def at_y(d):
        return (z * NY + lax.rem(y + NY + d, NY), rp)

    def at_x(i):
        return (ex, lax.rem(x + NX + i, NX) * 4 + zl * 2 + core)

    pair = (ex, x * 4 + (1 - zl) * 2 + core)
    sibling = (ex, q * 2 + 1 - core)
    diagonal = (at_y(4)[0], pair[1])
    return z, x, zl, q, core, at_z, at_y, at_x, pair, sibling, diagonal


def remote(src, dst, send_sem, recv_sem, peer):
    return pltpu.make_async_remote_copy(
        src_ref=src, dst_ref=dst, send_sem=send_sem, recv_sem=recv_sem, device_id=peer, device_id_type=MESH
    )


def start(copies):
    for c in copies:
        c.start()


def slot(j, o):
    return pl.ds((ORDER.index(j) * 4 + o) * BLK, BLK)


def layer_kernel(scale, assign, tokens, cotangent, wg, wu, wd, grad_in, out_gate, out_up, out_down,
                 own, send, rows, w, down, pre, dh, dcat, hid, px, dw, theirs, from_pair, from_a, from_b, s2, from_z, s3, from_y,
                 s2d, from_d, mid, parts, sums, ret,
                 ls, zs, zr, ys, yr, ws, wr, ps, pr, hs, hr, cs, cr, as_, ar, bs, br, gs, gr, fs, fr):
    f32, bf = jnp.float32, jnp.bfloat16
    by_cols = (((1,), (1,)), ((), ()))
    by_rows = (((0,), (0,)), ((), ()))
    z, x, zl, q, core, at_z, at_y, at_x, pair, sibling, diagonal = place()

    peers = [at_z(i) for i in (1, 2, 3)] + [at_y(d) for d in (1, -1, 4)] + [at_x(i) for i in (1, 2, 3)] + [pair, sibling, diagonal]
    barrier = pltpu.get_barrier_semaphore()
    for peer in peers:
        pl.semaphore_signal(barrier, inc=1, device_id=peer, device_id_type=MESH)

    bring = [pltpu.make_async_copy(src, own.at[c], ls.at[3 + c]) for c, src in enumerate((tokens, cotangent))]
    start(bring)
    keep = [
        pltpu.make_async_copy(wg, w.at[:, 0:SLICE], ls.at[0]),
        pltpu.make_async_copy(wu, w.at[:, SLICE : 2 * SLICE], ls.at[1]),
        pltpu.make_async_copy(wd, down.at[0:SLICE], ls.at[2]),
    ]
    def select(c):
        bring[c].wait()
        first, second = own[c, 0:BLK], own[c, BLK : 2 * BLK]
        for e in range(E_WIN):
            other = jnp.where(assign[1] == e, second, jnp.zeros_like(second))
            send[c, e] = jnp.where(assign[0] == e, first, other)
        rows[c, slot(0, 0)] = send[c, z]

    pl.semaphore_wait(barrier, len(peers))

    half = pl.ds(pl.multiple_of(core * (D // 2), 128), D // 2)

    def weights(srcs, dsts, base, peer):
        return [remote(s, d, ws.at[base + n], wr.at[base + n], peer) for n, (s, d) in enumerate(zip(srcs, dsts))]

    def part(first, count):
        tall = pl.ds(pl.multiple_of(core * (D // 2) + first * ROWS, 32), count * ROWS)
        short = pl.ds(pl.multiple_of(SLICE + first * BLK, 16), count * BLK)
        return [w.at[tall, 2 * SLICE : 3 * SLICE], w.at[tall, 3 * SLICE : 4 * SLICE], down.at[short, half]]

    tall = pl.ds(pl.multiple_of(core * (D // 2) + q * ROWS, 32), ROWS)
    short = pl.ds(pl.multiple_of(q * BLK, 16), BLK)
    one, two, every = part(q, 1), part(2 * x, 2), part(0, 8)
    stage1 = weights([wg.at[tall], wu.at[tall], wd.at[short, half]], one, 0, at_y(4))
    stage2 = weights(one, one, 3, pair)
    stage3 = [weights(two, two, 6 + 3 * (i - 1), at_x(i)) for i in (1, 2, 3)]
    stage4 = weights(every, every, 15, sibling)

    by_z = {
        4 - i: [
            remote(send.at[c, lax.rem(z + i, E_WIN)], rows.at[c, slot(4 - i, 0)], zs.at[i - 1, c], zr.at[3 - i, c], at_z(i))
            for c in (0, 1)
        ]
        for i in (1, 2, 3)
    }

    def by_y(j, c):
        s = LEAN[j]
        return [
            remote(rows.at[c, slot(j, 0)], rows.at[c, slot(j, 1)], ys.at[j, 0, c], yr.at[j, 0, c], at_y(s)),
            remote(rows.at[c, slot(j, 0)], rows.at[c, slot(j, 2)], ys.at[j, 1, c], yr.at[j, 1, c], at_y(-s)),
            remote(rows.at[c, slot(j, 1)], rows.at[c, slot(j, 3)], ys.at[j, 2, c], yr.at[j, 2, c], at_y(s)),
        ]

    along_y = [[by_y(j, c) for c in (0, 1)] for j in range(E_WIN)]

    def spread(j, c):
        if j:
            by_z[j][c].wait_recv()
        start(along_y[j][c][:2])

    def relay(j, c):
        along_y[j][c][0].wait_recv()
        along_y[j][c][2].start()

    def landed(j):
        for c in (0, 1):
            along_y[j][c][1].wait_recv()
            along_y[j][c][2].wait_recv()

    def arrived(stage):
        for c in stage:
            c.wait_recv()

    def forward(lo, hi):
        pre[lo:hi] = jnp.zeros((hi - lo, 4 * SLICE), f32)
        dh[lo:hi] = jnp.zeros((hi - lo, 2 * SLICE), f32)

        @pl.loop(0, D // CHUNK)
        def _(n):
            cols = pl.ds(pl.multiple_of(n * CHUNK, 128), CHUNK)
            pre[lo:hi] += jnp.dot(rows[0, lo:hi, cols], w[cols, :], preferred_element_type=f32)
            dh[lo:hi] += lax.dot_general(rows[1, lo:hi, cols], down[:, cols], by_cols, preferred_element_type=f32)

    def pass_on(stage, n):
        if stage == 1:
            stage1[n].wait_recv()
            stage2[n].start()
        elif stage == 2:
            stage2[n].wait_recv()
            for group in stage3:
                group[n].start()
        else:
            for group in stage3:
                group[n].wait_recv()
            stage4[n].start()

    start(stage1)
    for c in (0, 1):
        select(c)
        by_z[3][c].start()
        by_z[1][c].start()
        spread(0, c)
    start(keep)
    pass_on(1, 0)
    relay(0, 0)
    start(by_z[2])
    pass_on(2, 0)
    pass_on(1, 1)
    spread(1, 0)
    spread(3, 0)
    relay(0, 1)
    pass_on(2, 1)
    pass_on(1, 2)
    spread(1, 1)
    spread(3, 1)
    pass_on(2, 2)
    relay(1, 0)
    relay(3, 0)
    pass_on(3, 0)
    relay(1, 1)
    relay(3, 1)
    spread(2, 0)
    pass_on(3, 1)
    spread(2, 1)
    relay(2, 0)
    pass_on(3, 2)
    relay(2, 1)
    for c in keep:
        c.wait()
    arrived(stage4)
    for j in ORDER[:3]:
        landed(j)
    forward(0, 3 * 64)
    landed(2)
    forward(3 * 64, N_ROWS)

    for h in (0, 1):
        a, b, c = 2 * h * SLICE, (2 * h + 1) * SLICE, (2 * h + 2) * SLICE
        gate, up, grad = pre[:, a:b], pre[:, b:c], dh[:, h * SLICE : (h + 1) * SLICE]
        sig = jax.nn.sigmoid(gate)
        silu = gate * sig
        hid[:, h * SLICE : (h + 1) * SLICE] = (silu * up).astype(bf)
        dcat[:, b:c] = (grad * silu).astype(bf)
        dcat[:, a:b] = (grad * up * sig * (1.0 + gate * (1.0 - sig))).astype(bf)

    near = {off: lax.rem(x + off, NX) for off in range(NX)}
    NEAR = (2, 1, 3, 0)
    LOW = ROWS // 2

    to_core = [
        {off: remote(dw.at[k, n, :, 1 - core], theirs.at[k, n], cs.at[k, off], cr.at[k, off], sibling) for off, n in near.items()}
        for k in range(3)
    ]
    first_pair = {off: remote(dw.at[0, n, 1 - zl, core], from_pair.at[n], gs.at[off], gr.at[off], pair) for off, n in near.items()}

    def piece(k, off, t):
        n = near[off]
        return dw.at[k, n, t, core] if k else dw.at[0, n, zl, core, LOW * t : LOW * (t + 1)]

    def in_a(k, t):
        return from_a.at[k, t] if k else from_a.at[0, t, 0:LOW]

    def in_b(k, side, t):
        return from_b.at[k, side, t] if k else from_b.at[0, side, t, 0:LOW]

    by_a = [
        [
            remote(piece(k, 2, 0), in_a(k, 0), as_.at[k, 0], ar.at[k, 0], at_x(1)),
            remote(piece(k, 2, 1), in_a(k, 1), as_.at[k, 1], ar.at[k, 1], at_x(-1)),
        ]
        for k in range(3)
    ]
    by_b = [
        [
            remote(piece(k, 1, 1), in_b(k, 0, 1), bs.at[k, 0], br.at[k, 0], at_x(1)),
            remote(piece(k, 3, 0), in_b(k, 1, 0), bs.at[k, 1], br.at[k, 1], at_x(-1)),
            remote(piece(k, 1, 0), in_b(k, 0, 0), bs.at[k, 2], br.at[k, 2], at_x(1)),
            remote(piece(k, 3, 1), in_b(k, 1, 1), bs.at[k, 3], br.at[k, 3], at_x(-1)),
        ]
        for k in range(3)
    ]
    to_pair = remote(s2.at[0, 1 - zl], from_z, gs.at[4], gr.at[4], pair)
    to_y = remote(s3, from_y, fs.at[0], fr.at[0], at_y(4))
    spread_down = [
        remote(s2d.at[1 - zl, 1], from_d.at[2], fs.at[3], fr.at[3], diagonal),
        remote(s2d.at[zl, 1], from_d.at[1], fs.at[2], fr.at[2], at_y(4)),
        remote(s2d.at[1 - zl, 0], from_d.at[0], fs.at[1], fr.at[1], pair),
    ]

    def weight_grad(k):
        for off in NEAR:
            n = near[off]
            cols = pl.ds(pl.multiple_of(n * CHUNK, 128), CHUNK)
            right = hid[...] if k == 2 else dcat[:, 2 * SLICE * k : 2 * SLICE * (k + 1)]
            full = lax.dot_general(rows[k // 2, :, cols], right, by_rows, preferred_element_type=f32)
            dw[k, n] = full.astype(bf).reshape(2, 2, ROWS, 2 * SLICE)
            to_core[k][off].start()

    def leave_x(k, off):
        if off == 2:
            start(by_a[k])
        elif off:
            by_b[k][off // 2].start()

    def over_cores(k):
        for off in NEAR:
            n = near[off]
            to_core[k][off].wait_recv()
            for t in (0, 1):
                dw[k, n, t, core] = (dw[k, n, t, core].astype(f32) + theirs[k, n, t].astype(f32)).astype(bf)
            if k:
                leave_x(k, off)
            else:
                first_pair[off].start()

    def over_pair_first():
        for off in NEAR:
            n = near[off]
            first_pair[off].wait_recv()
            dw[0, n, zl, core] = (dw[0, n, zl, core].astype(f32) + from_pair[n].astype(f32)).astype(bf)
            leave_x(0, off)

    def augment(k):
        for t, off in ((0, 1), (1, 3)):
            by_a[k][t].wait_recv()
            spot = piece(k, off, t)
            spot[...] = (spot[...].astype(f32) + in_a(k, t)[...].astype(f32)).astype(bf)
            by_b[k][2 + t].start()

    def x_total(k, t):
        return piece(k, 0, t)[...].astype(f32) + in_b(k, 0, t)[...].astype(f32) + in_b(k, 1, t)[...].astype(f32)

    def over_x(k):
        for c in by_b[k]:
            c.wait_recv()
        if k == 1:
            s2[0, 1 - zl] = x_total(1, 1 - zl).astype(bf)
            to_pair.start()
            s2[0, zl] = x_total(1, zl).astype(bf)
        elif k == 2:
            for t in (1 - zl, zl):
                total = x_total(2, t).astype(bf)
                s2d[t, 0] = total[:, :SLICE]
                s2d[t, 1] = total[:, SLICE:]
            start(spread_down)
        else:
            for t in (0, 1):
                total = x_total(0, t) * scale
                out_gate[LOW * t : LOW * (t + 1)] = total[:, :SLICE]
                out_up[LOW * t : LOW * (t + 1)] = total[:, SLICE:]

    def over_pair():
        to_pair.wait_recv()
        s3[...] = (s2[0, zl].astype(f32) + from_z[...].astype(f32)).astype(bf)
        to_y.start()

    def finish():
        to_y.wait_recv()
        out_gate[...] += from_y[:, :SLICE].astype(f32) * scale
        out_up[...] += from_y[:, SLICE:].astype(f32) * scale
        arrived(spread_down)
        total = s2d[zl, 0].astype(f32)
        for n in range(3):
            total += from_d[n].astype(f32)
        out_down[...] = total * scale

    def backward(j):
        s = LEAN[j]
        return [
            remote(px.at[slot(j, 3)], mid.at[j], ps.at[j, 0], pr.at[j, 0], at_y(-s)),
            remote(px.at[slot(j, 2)], parts.at[j, 1], ps.at[j, 1], pr.at[j, 1], at_y(s)),
            remote(px.at[slot(j, 1)], parts.at[j, 0], ps.at[j, 2], pr.at[j, 2], at_y(-s)),
        ]

    back = [backward(j) for j in range(E_WIN)]
    home = {j: remote(sums.at[j], ret.at[z], hs.at[j - 1], hr.at[j - 1], at_z(j)) for j in (1, 2, 3)}
    landing = {j: remote(sums.at[j], ret.at[lax.rem(z + 4 - j, E_WIN)], hs.at[j - 1], hr.at[j - 1], at_z(j)) for j in (1, 2, 3)}

    def input_grad():
        @pl.loop(0, D // CHUNK)
        def _(n):
            cols = pl.ds(pl.multiple_of(n * CHUNK, 128), CHUNK)
            px[:, cols] = lax.dot_general(dcat[...], w[cols, :], by_cols, preferred_element_type=f32).astype(bf)

        for j in (2, 1, 3, 0):
            start(back[j][:2])

    def meet(j):
        back[j][0].wait_recv()
        spot = slot(j, 1)
        px[spot] = (px[spot].astype(f32) + mid[j].astype(f32)).astype(bf)
        back[j][2].start()

    def gather(j):
        arrived(back[j][1:])
        total = px[slot(j, 0)].astype(f32) + parts[j, 0].astype(f32) + parts[j, 1].astype(f32)
        if j:
            sums[j] = total.astype(bf)
            home[j].start()
        else:
            ret[z] = total.astype(bf)

    weight_grad(1)
    weight_grad(0)
    over_cores(1)
    input_grad()
    over_cores(0)
    weight_grad(2)
    augment(1)
    over_cores(2)
    for j in (2, 1, 3, 0):
        meet(j)
    over_x(1)
    augment(2)
    over_pair()
    over_pair_first()
    gather(2)
    over_x(2)
    augment(0)
    gather(1)
    gather(3)
    gather(0)
    over_x(0)
    finish()

    for j in (1, 2, 3):
        landing[j].wait_recv()
    for b in (0, 1):
        mine = ret[0]
        for e in range(1, E_WIN):
            mine = jnp.where(assign[b] == e, ret[e], mine)
        grad_in[b * BLK : (b + 1) * BLK] = mine

    groups = list(by_z.values()) + [g for both in along_y for g in both] + stage3 + [stage1, stage2, stage4]
    groups += back + by_a + by_b + [[to_pair, to_y], spread_down] + [list(g.values()) for g in to_core + [first_pair, home]]
    for group in groups:
        for c in group:
            c.wait_send()


def layer(assign, tokens, cotangent, wg, wu, wd, scale):
    f32, bf = jnp.float32, jnp.bfloat16
    dma = pltpu.SemaphoreType.DMA
    anywhere = pl.BlockSpec(memory_space=pl.ANY)
    vmem = pl.BlockSpec(memory_space=pltpu.VMEM)
    return pl.pallas_call(
        functools.partial(layer_kernel, scale),
        out_shape=(
            jax.ShapeDtypeStruct((2 * BLK, D), bf),
            jax.ShapeDtypeStruct((ROWS, SLICE), f32),
            jax.ShapeDtypeStruct((ROWS, SLICE), f32),
            jax.ShapeDtypeStruct((ROWS, SLICE), f32),
        ),
        in_specs=[pl.BlockSpec(memory_space=pltpu.SMEM)] + [anywhere] * 5,
        out_specs=(vmem, vmem, vmem, vmem),
        scratch_shapes=[
            pltpu.VMEM((2, 2 * BLK, D), bf),
            pltpu.VMEM((2, E_WIN, BLK, D), bf),
            pltpu.VMEM((2, N_ROWS, D), bf),
            pltpu.VMEM((D, 4 * SLICE), bf),
            pltpu.VMEM((2 * SLICE, D), bf),
            pltpu.VMEM((N_ROWS, 4 * SLICE), f32),
            pltpu.VMEM((N_ROWS, 2 * SLICE), f32),
            pltpu.VMEM((N_ROWS, 4 * SLICE), bf),
            pltpu.VMEM((N_ROWS, 2 * SLICE), bf),
            pltpu.VMEM((N_ROWS, D), bf),
            pltpu.VMEM((3, NX, 2, 2, ROWS, 2 * SLICE), bf),
            pltpu.VMEM((3, NX, 2, ROWS, 2 * SLICE), bf),
            pltpu.VMEM((NX, ROWS, 2 * SLICE), bf),
            pltpu.VMEM((3, 2, ROWS, 2 * SLICE), bf),
            pltpu.VMEM((3, 2, 2, ROWS, 2 * SLICE), bf),
            pltpu.VMEM((1, 2, ROWS, 2 * SLICE), bf),
            pltpu.VMEM((ROWS, 2 * SLICE), bf),
            pltpu.VMEM((ROWS, 2 * SLICE), bf),
            pltpu.VMEM((ROWS, 2 * SLICE), bf),
            pltpu.VMEM((2, 2, ROWS, SLICE), bf),
            pltpu.VMEM((3, ROWS, SLICE), bf),
            pltpu.VMEM((E_WIN, BLK, D), bf),
            pltpu.VMEM((E_WIN, 2, BLK, D), bf),
            pltpu.VMEM((E_WIN, BLK, D), bf),
            pltpu.VMEM((E_WIN, BLK, D), bf),
            dma((5,)),
            dma((3, 2)), dma((3, 2)),
            dma((4, 3, 2)), dma((4, 3, 2)),
            dma((18,)), dma((18,)),
            dma((4, 3)), dma((4, 3)),
            dma((3,)), dma((3,)),
            dma((3, 4)), dma((3, 4)),
            dma((3, 2)), dma((3, 2)),
            dma((3, 4)), dma((3, 4)),
            dma((5,)), dma((5,)),
            dma((4,)), dma((4,)),
        ],
        compiler_params=pltpu.CompilerParams(collective_id=0, has_side_effects=True, vmem_limit_bytes=56 * 2**20),
        cost_estimate=pl.CostEstimate(flops=16 * N_ROWS * D * 2 * SLICE, bytes_accessed=2**24, transcendentals=0),
        name="layer",
    )(assign, tokens, cotangent, wg, wu, wd)


def hand_over_kernel(*refs):
    sems = refs[-1]
    copies = [pltpu.make_async_copy(refs[n], refs[4 + n], sems.at[n]) for n in range(4)]
    start(copies)
    for c in copies:
        c.wait()


def hand_over(*arrays):
    hbm = pl.BlockSpec(memory_space=pltpu.HBM)
    return pl.pallas_call(
        hand_over_kernel,
        out_shape=tuple(jax.ShapeDtypeStruct(a.shape, a.dtype) for a in arrays),
        in_specs=[hbm] * 4,
        out_specs=[hbm] * 4,
        scratch_shapes=[pltpu.SemaphoreType.DMA((4,))],
        name="hand_over",
    )(*arrays)


def shards(tokens, cotangent, assign, w_gate, w_up, w_down):
    scale = 1.0 / math.sqrt(lax.axis_size("expert") * lax.axis_size("replica") * BLK // 2)
    grad_in, gate, up, down = hand_over(*layer(assign, tokens, cotangent, w_gate, w_up, w_down, scale))
    return grad_in, gate, up, jnp.transpose(down)


def solution(mesh):
    placed = (
        P(("expert", "replica"), None),
        P(("expert", "replica"), None),
        P(("expert", "replica")),
        P(None, "expert"),
        P(None, "expert"),
        P("expert", None),
    )
    return jax.shard_map(
        shards,
        mesh=mesh,
        in_specs=placed,
        out_specs=(
            P(("expert", "replica"), None),
            P("replica", "expert"),
            P("replica", "expert"),
            P("expert", "replica"),
        ),
        check_vma=False,
    )
```

```python
import functools
import math

import jax
import jax.numpy as jnp
from jax import lax
from jax.experimental import pallas as pl
from jax.experimental.pallas import tpu as pltpu
from jax.sharding import PartitionSpec as P

E_WIN = 4
NY = 8
NX = 4
BLK = 16
D = 3584
SLICE = 128
ROWS = 224
CHUNK = 896
N_ROWS = 256
MESH = pl.DeviceIdType.MESH
LEAN = (1, -1, -1, 1)
ORDER = (0, 1, 3, 2)


def place():
    ex = lax.axis_index("expert")
    rp = lax.axis_index("replica")
    z, y = lax.div(ex, NY), lax.rem(ex, NY)
    q, core = lax.div(rp, 2), lax.rem(rp, 2)
    x, zl = lax.div(q, 2), lax.rem(q, 2)

    def at_z(i):
        return (lax.rem(z + i, E_WIN) * NY + y, rp)

    def at_y(d):
        return (z * NY + lax.rem(y + NY + d, NY), rp)

    def at_x(i):
        return (ex, lax.rem(x + NX + i, NX) * 4 + zl * 2 + core)

    pair = (ex, x * 4 + (1 - zl) * 2 + core)
    sibling = (ex, q * 2 + 1 - core)
    diagonal = (at_y(4)[0], pair[1])
    return z, x, zl, q, core, at_z, at_y, at_x, pair, sibling, diagonal


def remote(src, dst, send_sem, recv_sem, peer):
    return pltpu.make_async_remote_copy(
        src_ref=src, dst_ref=dst, send_sem=send_sem, recv_sem=recv_sem, device_id=peer, device_id_type=MESH
    )


def start(copies):
    for c in copies:
        c.start()


def slot(j, o):
    return pl.ds((ORDER.index(j) * 4 + o) * BLK, BLK)


def layer_kernel(scale, assign, tokens, cotangent, wg, wu, wd, grad_in, out_gate, out_up, out_down,
                 own, send, rows, w, down, pre, dh, dcat, hid, px, dw, theirs, from_pair, from_a, from_b, s2, from_z, s3, from_y,
                 s2d, from_d, mid, parts, sums, ret,
                 ls, zs, zr, ys, yr, ws, wr, ps, pr, hs, hr, cs, cr, as_, ar, bs, br, gs, gr, fs, fr):
    f32, bf = jnp.float32, jnp.bfloat16
    by_cols = (((1,), (1,)), ((), ()))
    by_rows = (((0,), (0,)), ((), ()))
    z, x, zl, q, core, at_z, at_y, at_x, pair, sibling, diagonal = place()

    peers = [at_z(i) for i in (1, 2, 3)] + [at_y(d) for d in (1, -1, 4)] + [at_x(i) for i in (1, 2, 3)] + [pair, sibling, diagonal]
    barrier = pltpu.get_barrier_semaphore()
    for peer in peers:
        pl.semaphore_signal(barrier, inc=1, device_id=peer, device_id_type=MESH)

    bring = [pltpu.make_async_copy(src, own.at[c], ls.at[3 + c]) for c, src in enumerate((tokens, cotangent))]
    start(bring)
    keep = [
        pltpu.make_async_copy(wg, w.at[:, 0:SLICE], ls.at[0]),
        pltpu.make_async_copy(wu, w.at[:, SLICE : 2 * SLICE], ls.at[1]),
        pltpu.make_async_copy(wd, down.at[0:SLICE], ls.at[2]),
    ]
    def select(c):
        bring[c].wait()
        first, second = own[c, 0:BLK], own[c, BLK : 2 * BLK]
        for e in range(E_WIN):
            other = jnp.where(assign[1] == e, second, jnp.zeros_like(second))
            send[c, e] = jnp.where(assign[0] == e, first, other)
        rows[c, slot(0, 0)] = send[c, z]

    half = pl.ds(pl.multiple_of(core * (D // 2), 128), D // 2)

    def weights(srcs, dsts, base, peer):
        return [remote(s, d, ws.at[base + n], wr.at[base + n], peer) for n, (s, d) in enumerate(zip(srcs, dsts))]

    def part(first, count):
        tall = pl.ds(pl.multiple_of(core * (D // 2) + first * ROWS, 32), count * ROWS)
        short = pl.ds(pl.multiple_of(SLICE + first * BLK, 16), count * BLK)
        return [w.at[tall, 2 * SLICE : 3 * SLICE], w.at[tall, 3 * SLICE : 4 * SLICE], down.at[short, half]]

    tall = pl.ds(pl.multiple_of(core * (D // 2) + q * ROWS, 32), ROWS)
    short = pl.ds(pl.multiple_of(q * BLK, 16), BLK)
    one, two, every = part(q, 1), part(2 * x, 2), part(0, 8)
    stage1 = weights([wg.at[tall], wu.at[tall], wd.at[short, half]], one, 0, at_y(4))
    stage2 = weights(one, one, 3, pair)
    stage3 = [weights(two, two, 6 + 3 * (i - 1), at_x(i)) for i in (1, 2, 3)]
    stage4 = weights(every, every, 15, sibling)

    by_z = {
        4 - i: [
            remote(send.at[c, lax.rem(z + i, E_WIN)], rows.at[c, slot(4 - i, 0)], zs.at[i - 1, c], zr.at[3 - i, c], at_z(i))
            for c in (0, 1)
        ]
        for i in (1, 2, 3)
    }

    def by_y(j, c):
        s = LEAN[j]
        return [
            remote(rows.at[c, slot(j, 0)], rows.at[c, slot(j, 1)], ys.at[j, 0, c], yr.at[j, 0, c], at_y(s)),
            remote(rows.at[c, slot(j, 0)], rows.at[c, slot(j, 2)], ys.at[j, 1, c], yr.at[j, 1, c], at_y(-s)),
            remote(rows.at[c, slot(j, 1)], rows.at[c, slot(j, 3)], ys.at[j, 2, c], yr.at[j, 2, c], at_y(s)),
        ]

    along_y = [[by_y(j, c) for c in (0, 1)] for j in range(E_WIN)]

    def spread(j, c):
        if j:
            by_z[j][c].wait_recv()
        start(along_y[j][c][:2])

    def relay(j, c):
        along_y[j][c][0].wait_recv()
        along_y[j][c][2].start()

    def landed(j):
        for c in (0, 1):
            along_y[j][c][1].wait_recv()
            along_y[j][c][2].wait_recv()

    def arrived(stage):
        for c in stage:
            c.wait_recv()

    def forward(lo, hi):
        pre[lo:hi] = jnp.zeros((hi - lo, 4 * SLICE), f32)
        dh[lo:hi] = jnp.zeros((hi - lo, 2 * SLICE), f32)

        @pl.loop(0, D // CHUNK)
        def _(n):
            cols = pl.ds(pl.multiple_of(n * CHUNK, 128), CHUNK)
            pre[lo:hi] += jnp.dot(rows[0, lo:hi, cols], w[cols, :], preferred_element_type=f32)
            dh[lo:hi] += lax.dot_general(rows[1, lo:hi, cols], down[:, cols], by_cols, preferred_element_type=f32)

    def pass_on(stage, n):
        if stage == 1:
            stage1[n].wait_recv()
            stage2[n].start()
        elif stage == 2:
            stage2[n].wait_recv()
            for group in stage3:
                group[n].start()
        else:
            for group in stage3:
                group[n].wait_recv()
            stage4[n].start()

    pl.semaphore_wait(barrier, len(peers))
    start(stage1)
    select(0)
    by_z[3][0].start()
    by_z[1][0].start()
    spread(0, 0)
    select(1)
    by_z[3][1].start()
    by_z[1][1].start()
    spread(0, 1)
    start(keep)
    pass_on(1, 0)
    relay(0, 0)
    pass_on(2, 0)
    pass_on(1, 1)
    relay(0, 1)
    by_z[2][0].start()
    by_z[2][1].start()
    spread(1, 0)
    spread(3, 0)
    pass_on(2, 1)
    pass_on(1, 2)
    spread(1, 1)
    spread(3, 1)
    pass_on(2, 2)
    relay(1, 0)
    relay(3, 0)
    pass_on(3, 0)
    relay(1, 1)
    relay(3, 1)
    spread(2, 0)
    pass_on(3, 1)
    spread(2, 1)
    relay(2, 0)
    pass_on(3, 2)
    relay(2, 1)
    for c in keep:
        c.wait()
    arrived(stage4)
    for j in ORDER[:3]:
        landed(j)
    forward(0, 3 * 64)
    landed(2)
    forward(3 * 64, N_ROWS)

    for h in (0, 1):
        a, b, c = 2 * h * SLICE, (2 * h + 1) * SLICE, (2 * h + 2) * SLICE
        gate, up, grad = pre[:, a:b], pre[:, b:c], dh[:, h * SLICE : (h + 1) * SLICE]
        sig = jax.nn.sigmoid(gate)
        silu = gate * sig
        hid[:, h * SLICE : (h + 1) * SLICE] = (silu * up).astype(bf)
        dcat[:, b:c] = (grad * silu).astype(bf)
        dcat[:, a:b] = (grad * up * sig * (1.0 + gate * (1.0 - sig))).astype(bf)

    near = {off: lax.rem(x + off, NX) for off in range(NX)}
    NEAR = (2, 1, 3, 0)
    LOW = ROWS // 2

    to_core = [
        {off: remote(dw.at[k, n, :, 1 - core], theirs.at[k, n], cs.at[k, off], cr.at[k, off], sibling) for off, n in near.items()}
        for k in range(3)
    ]
    first_pair = {off: remote(dw.at[0, n, 1 - zl, core], from_pair.at[n], gs.at[off], gr.at[off], pair) for off, n in near.items()}

    def piece(k, off, t):
        n = near[off]
        return dw.at[k, n, t, core] if k else dw.at[0, n, zl, core, LOW * t : LOW * (t + 1)]

    def in_a(k, t):
        return from_a.at[k, t] if k else from_a.at[0, t, 0:LOW]

    def in_b(k, side, t):
        return from_b.at[k, side, t] if k else from_b.at[0, side, t, 0:LOW]

    by_a = [
        [
            remote(piece(k, 2, 0), in_a(k, 0), as_.at[k, 0], ar.at[k, 0], at_x(1)),
            remote(piece(k, 2, 1), in_a(k, 1), as_.at[k, 1], ar.at[k, 1], at_x(-1)),
        ]
        for k in range(3)
    ]
    by_b = [
        [
            remote(piece(k, 1, 1), in_b(k, 0, 1), bs.at[k, 0], br.at[k, 0], at_x(1)),
            remote(piece(k, 3, 0), in_b(k, 1, 0), bs.at[k, 1], br.at[k, 1], at_x(-1)),
            remote(piece(k, 1, 0), in_b(k, 0, 0), bs.at[k, 2], br.at[k, 2], at_x(1)),
            remote(piece(k, 3, 1), in_b(k, 1, 1), bs.at[k, 3], br.at[k, 3], at_x(-1)),
        ]
        for k in range(3)
    ]
    to_pair = remote(s2.at[0, 1 - zl], from_z, gs.at[4], gr.at[4], pair)
    to_y = remote(s3, from_y, fs.at[0], fr.at[0], at_y(4))
    spread_down = [
        remote(s2d.at[1 - zl, 1], from_d.at[2], fs.at[3], fr.at[3], diagonal),
        remote(s2d.at[zl, 1], from_d.at[1], fs.at[2], fr.at[2], at_y(4)),
        remote(s2d.at[1 - zl, 0], from_d.at[0], fs.at[1], fr.at[1], pair),
    ]

    def weight_grad(k):
        for off in NEAR:
            n = near[off]
            cols = pl.ds(pl.multiple_of(n * CHUNK, 128), CHUNK)
            right = hid[...] if k == 2 else dcat[:, 2 * SLICE * k : 2 * SLICE * (k + 1)]
            full = lax.dot_general(rows[k // 2, :, cols], right, by_rows, preferred_element_type=f32)
            dw[k, n] = full.astype(bf).reshape(2, 2, ROWS, 2 * SLICE)
            to_core[k][off].start()

    def leave_x(k, off):
        if off == 2:
            start(by_a[k])
        elif off and k == 0:
            by_b[k][off // 2].start()

    def rest(k):
        start(by_b[k][:2])

    def over_cores(k):
        for off in NEAR:
            n = near[off]
            to_core[k][off].wait_recv()
            for t in (0, 1):
                dw[k, n, t, core] = (dw[k, n, t, core].astype(f32) + theirs[k, n, t].astype(f32)).astype(bf)
            if k:
                leave_x(k, off)
            else:
                first_pair[off].start()

    def over_pair_first():
        for off in NEAR:
            n = near[off]
            first_pair[off].wait_recv()
            dw[0, n, zl, core] = (dw[0, n, zl, core].astype(f32) + from_pair[n].astype(f32)).astype(bf)
            leave_x(0, off)

    def augment(k):
        for t, off in ((0, 1), (1, 3)):
            by_a[k][t].wait_recv()
            spot = piece(k, off, t)
            spot[...] = (spot[...].astype(f32) + in_a(k, t)[...].astype(f32)).astype(bf)
            by_b[k][2 + t].start()

    def x_total(k, t):
        return piece(k, 0, t)[...].astype(f32) + in_b(k, 0, t)[...].astype(f32) + in_b(k, 1, t)[...].astype(f32)

    def over_x(k):
        for c in by_b[k]:
            c.wait_recv()
        if k == 1:
            s2[0, 1 - zl] = x_total(1, 1 - zl).astype(bf)
            to_pair.start()
            s2[0, zl] = x_total(1, zl).astype(bf)
        elif k == 2:
            for t in (1 - zl, zl):
                total = x_total(2, t).astype(bf)
                s2d[t, 0] = total[:, :SLICE]
                s2d[t, 1] = total[:, SLICE:]
            start(spread_down)
        else:
            for t in (0, 1):
                total = x_total(0, t) * scale
                out_gate[LOW * t : LOW * (t + 1)] = total[:, :SLICE]
                out_up[LOW * t : LOW * (t + 1)] = total[:, SLICE:]

    def over_pair():
        to_pair.wait_recv()
        s3[...] = (s2[0, zl].astype(f32) + from_z[...].astype(f32)).astype(bf)
        to_y.start()

    def finish():
        to_y.wait_recv()
        out_gate[...] += from_y[:, :SLICE].astype(f32) * scale
        out_up[...] += from_y[:, SLICE:].astype(f32) * scale
        arrived(spread_down)
        total = s2d[zl, 0].astype(f32)
        for n in range(3):
            total += from_d[n].astype(f32)
        out_down[...] = total * scale

    def backward(j):
        s = LEAN[j]
        return [
            remote(px.at[slot(j, 3)], mid.at[j], ps.at[j, 0], pr.at[j, 0], at_y(-s)),
            remote(px.at[slot(j, 2)], parts.at[j, 1], ps.at[j, 1], pr.at[j, 1], at_y(s)),
            remote(px.at[slot(j, 1)], parts.at[j, 0], ps.at[j, 2], pr.at[j, 2], at_y(-s)),
        ]

    back = [backward(j) for j in range(E_WIN)]
    home = {j: remote(sums.at[j], ret.at[z], hs.at[j - 1], hr.at[j - 1], at_z(j)) for j in (1, 2, 3)}
    landing = {j: remote(sums.at[j], ret.at[lax.rem(z + 4 - j, E_WIN)], hs.at[j - 1], hr.at[j - 1], at_z(j)) for j in (1, 2, 3)}

    def input_grad():
        @pl.loop(0, D // CHUNK)
        def _(n):
            cols = pl.ds(pl.multiple_of(n * CHUNK, 128), CHUNK)
            px[:, cols] = lax.dot_general(dcat[...], w[cols, :], by_cols, preferred_element_type=f32).astype(bf)

    def leave(j):
        start(back[j][:2])

    def meet(j):
        back[j][0].wait_recv()
        spot = slot(j, 1)
        px[spot] = (px[spot].astype(f32) + mid[j].astype(f32)).astype(bf)
        back[j][2].start()

    def gather(j):
        arrived(back[j][1:])
        total = px[slot(j, 0)].astype(f32) + parts[j, 0].astype(f32) + parts[j, 1].astype(f32)
        if j:
            sums[j] = total.astype(bf)
            home[j].start()
        else:
            ret[z] = total.astype(bf)

    input_grad()
    leave(2)
    weight_grad(1)
    leave(1)
    weight_grad(0)
    leave(3)
    over_cores(1)
    rest(1)
    leave(0)
    over_cores(0)
    meet(2)
    weight_grad(2)
    augment(1)
    meet(1)
    over_cores(2)
    rest(2)
    meet(3)
    augment(2)
    meet(0)
    over_x(1)
    gather(2)
    over_pair_first()
    over_pair()
    gather(1)
    over_x(2)
    augment(0)
    gather(3)
    gather(0)
    over_x(0)
    finish()

    for j in (1, 2, 3):
        landing[j].wait_recv()
    for b in (0, 1):
        mine = ret[0]
        for e in range(1, E_WIN):
            mine = jnp.where(assign[b] == e, ret[e], mine)
        grad_in[b * BLK : (b + 1) * BLK] = mine

    groups = list(by_z.values()) + [g for both in along_y for g in both] + stage3 + [stage1, stage2, stage4]
    groups += back + by_a + by_b + [[to_pair, to_y], spread_down] + [list(g.values()) for g in to_core + [first_pair, home]]
    for group in groups:
        for c in group:
            c.wait_send()


def layer(assign, tokens, cotangent, wg, wu, wd, scale):
    f32, bf = jnp.float32, jnp.bfloat16
    dma = pltpu.SemaphoreType.DMA
    anywhere = pl.BlockSpec(memory_space=pl.ANY)
    vmem = pl.BlockSpec(memory_space=pltpu.VMEM)
    return pl.pallas_call(
        functools.partial(layer_kernel, scale),
        out_shape=(
            jax.ShapeDtypeStruct((2 * BLK, D), bf),
            jax.ShapeDtypeStruct((ROWS, SLICE), f32),
            jax.ShapeDtypeStruct((ROWS, SLICE), f32),
            jax.ShapeDtypeStruct((ROWS, SLICE), f32),
        ),
        in_specs=[pl.BlockSpec(memory_space=pltpu.SMEM)] + [anywhere] * 5,
        out_specs=(vmem, vmem, vmem, vmem),
        scratch_shapes=[
            pltpu.VMEM((2, 2 * BLK, D), bf),
            pltpu.VMEM((2, E_WIN, BLK, D), bf),
            pltpu.VMEM((2, N_ROWS, D), bf),
            pltpu.VMEM((D, 4 * SLICE), bf),
            pltpu.VMEM((2 * SLICE, D), bf),
            pltpu.VMEM((N_ROWS, 4 * SLICE), f32),
            pltpu.VMEM((N_ROWS, 2 * SLICE), f32),
            pltpu.VMEM((N_ROWS, 4 * SLICE), bf),
            pltpu.VMEM((N_ROWS, 2 * SLICE), bf),
            pltpu.VMEM((N_ROWS, D), bf),
            pltpu.VMEM((3, NX, 2, 2, ROWS, 2 * SLICE), bf),
            pltpu.VMEM((3, NX, 2, ROWS, 2 * SLICE), bf),
            pltpu.VMEM((NX, ROWS, 2 * SLICE), bf),
            pltpu.VMEM((3, 2, ROWS, 2 * SLICE), bf),
            pltpu.VMEM((3, 2, 2, ROWS, 2 * SLICE), bf),
            pltpu.VMEM((1, 2, ROWS, 2 * SLICE), bf),
            pltpu.VMEM((ROWS, 2 * SLICE), bf),
            pltpu.VMEM((ROWS, 2 * SLICE), bf),
            pltpu.VMEM((ROWS, 2 * SLICE), bf),
            pltpu.VMEM((2, 2, ROWS, SLICE), bf),
            pltpu.VMEM((3, ROWS, SLICE), bf),
            pltpu.VMEM((E_WIN, BLK, D), bf),
            pltpu.VMEM((E_WIN, 2, BLK, D), bf),
            pltpu.VMEM((E_WIN, BLK, D), bf),
            pltpu.VMEM((E_WIN, BLK, D), bf),
            dma((5,)),
            dma((3, 2)), dma((3, 2)),
            dma((4, 3, 2)), dma((4, 3, 2)),
            dma((18,)), dma((18,)),
            dma((4, 3)), dma((4, 3)),
            dma((3,)), dma((3,)),
            dma((3, 4)), dma((3, 4)),
            dma((3, 2)), dma((3, 2)),
            dma((3, 4)), dma((3, 4)),
            dma((5,)), dma((5,)),
            dma((4,)), dma((4,)),
        ],
        compiler_params=pltpu.CompilerParams(collective_id=0, has_side_effects=True, vmem_limit_bytes=56 * 2**20),
        cost_estimate=pl.CostEstimate(flops=16 * N_ROWS * D * 2 * SLICE, bytes_accessed=2**24, transcendentals=0),
        name="layer",
    )(assign, tokens, cotangent, wg, wu, wd)


def hand_over_kernel(*refs):
    for n in range(4):
        refs[4 + n][...] = refs[n][...]


def hand_over(*arrays):
    vmem = pl.BlockSpec(memory_space=pltpu.VMEM)
    return pl.pallas_call(
        hand_over_kernel,
        out_shape=tuple(jax.ShapeDtypeStruct(a.shape, a.dtype) for a in arrays),
        in_specs=[vmem] * 4,
        out_specs=[vmem] * 4,
        name="hand_over",
    )(*arrays)


def shards(tokens, cotangent, assign, w_gate, w_up, w_down):
    scale = 1.0 / math.sqrt(lax.axis_size("expert") * lax.axis_size("replica") * BLK // 2)
    grad_in, gate, up, down = hand_over(*layer(assign, tokens, cotangent, w_gate, w_up, w_down, scale))
    return grad_in, gate, up, jnp.transpose(down)


def solution(mesh):
    placed = (
        P(("expert", "replica"), None),
        P(("expert", "replica"), None),
        P(("expert", "replica")),
        P(None, "expert"),
        P(None, "expert"),
        P("expert", None),
    )
    return jax.shard_map(
        shards,
        mesh=mesh,
        in_specs=placed,
        out_specs=(
            P(("expert", "replica"), None),
            P("replica", "expert"),
            P("replica", "expert"),
            P("expert", "replica"),
        ),
        check_vma=False,
    )
```

```python
import functools
import math

import jax
import jax.numpy as jnp
from jax import lax
from jax.experimental import pallas as pl
from jax.experimental.pallas import tpu as pltpu
from jax.sharding import PartitionSpec as P

E_WIN = 4
NY = 8
NX = 4
BLK = 16
D = 3584
SLICE = 128
ROWS = 224
CHUNK = 896
N_ROWS = 256
MESH = pl.DeviceIdType.MESH
LEAN = (1, -1, -1, 1)
ORDER = (0, 1, 3, 2)


def place():
    ex = lax.axis_index("expert")
    rp = lax.axis_index("replica")
    z, y = lax.div(ex, NY), lax.rem(ex, NY)
    q, core = lax.div(rp, 2), lax.rem(rp, 2)
    x, zl = lax.div(q, 2), lax.rem(q, 2)

    def at_z(i):
        return (lax.rem(z + i, E_WIN) * NY + y, rp)

    def at_y(d):
        return (z * NY + lax.rem(y + NY + d, NY), rp)

    def at_x(i):
        return (ex, lax.rem(x + NX + i, NX) * 4 + zl * 2 + core)

    pair = (ex, x * 4 + (1 - zl) * 2 + core)
    sibling = (ex, q * 2 + 1 - core)
    diagonal = (at_y(4)[0], pair[1])
    return z, x, zl, q, core, at_z, at_y, at_x, pair, sibling, diagonal


def remote(src, dst, send_sem, recv_sem, peer):
    return pltpu.make_async_remote_copy(
        src_ref=src, dst_ref=dst, send_sem=send_sem, recv_sem=recv_sem, device_id=peer, device_id_type=MESH
    )


def start(copies):
    for c in copies:
        c.start()


def slot(j, o):
    return pl.ds((ORDER.index(j) * 4 + o) * BLK, BLK)


def layer_kernel(scale, assign, tokens, cotangent, wg, wu, wd, grad_in, out_gate, out_up, out_down,
                 own, send, rows, w, down, pre, dh, dcat, hid, px, dw, theirs, from_pair, from_a, from_b, s2, from_z, s3, from_y,
                 s2d, from_d, mid, parts, sums, ret,
                 ls, zs, zr, ys, yr, ws, wr, ps, pr, hs, hr, cs, cr, as_, ar, bs, br, gs, gr, fs, fr):
    f32, bf = jnp.float32, jnp.bfloat16
    by_cols = (((1,), (1,)), ((), ()))
    by_rows = (((0,), (0,)), ((), ()))
    z, x, zl, q, core, at_z, at_y, at_x, pair, sibling, diagonal = place()

    peers = [at_z(i) for i in (1, 2, 3)] + [at_y(d) for d in (1, -1, 4)] + [at_x(i) for i in (1, 2, 3)] + [pair, sibling, diagonal]
    barrier = pltpu.get_barrier_semaphore()
    for peer in peers:
        pl.semaphore_signal(barrier, inc=1, device_id=peer, device_id_type=MESH)

    bring = [pltpu.make_async_copy(src, own.at[c], ls.at[3 + c]) for c, src in enumerate((tokens, cotangent))]
    start(bring)
    keep = [
        pltpu.make_async_copy(wg, w.at[:, 0:SLICE], ls.at[0]),
        pltpu.make_async_copy(wu, w.at[:, SLICE : 2 * SLICE], ls.at[1]),
        pltpu.make_async_copy(wd, down.at[0:SLICE], ls.at[2]),
    ]
    def select(c):
        bring[c].wait()
        first, second = own[c, 0:BLK], own[c, BLK : 2 * BLK]
        for e in range(E_WIN):
            other = jnp.where(assign[1] == e, second, jnp.zeros_like(second))
            send[c, e] = jnp.where(assign[0] == e, first, other)
        rows[c, slot(0, 0)] = send[c, z]

    half = pl.ds(pl.multiple_of(core * (D // 2), 128), D // 2)

    def weights(srcs, dsts, base, peer):
        return [remote(s, d, ws.at[base + n], wr.at[base + n], peer) for n, (s, d) in enumerate(zip(srcs, dsts))]

    def part(first, count):
        tall = pl.ds(pl.multiple_of(core * (D // 2) + first * ROWS, 32), count * ROWS)
        short = pl.ds(pl.multiple_of(SLICE + first * BLK, 16), count * BLK)
        return [w.at[tall, 2 * SLICE : 3 * SLICE], w.at[tall, 3 * SLICE : 4 * SLICE], down.at[short, half]]

    tall = pl.ds(pl.multiple_of(core * (D // 2) + q * ROWS, 32), ROWS)
    short = pl.ds(pl.multiple_of(q * BLK, 16), BLK)
    one, two, every = part(q, 1), part(2 * x, 2), part(0, 8)
    stage1 = weights([wg.at[tall], wu.at[tall], wd.at[short, half]], one, 0, at_y(4))
    stage2 = weights(one, one, 3, pair)
    stage3 = [weights(two, two, 6 + 3 * (i - 1), at_x(i)) for i in (1, 2, 3)]
    stage4 = weights(every, every, 15, sibling)

    by_z = {
        4 - i: [
            remote(send.at[c, lax.rem(z + i, E_WIN)], rows.at[c, slot(4 - i, 0)], zs.at[i - 1, c], zr.at[3 - i, c], at_z(i))
            for c in (0, 1)
        ]
        for i in (1, 2, 3)
    }

    def by_y(j, c):
        s = LEAN[j]
        return [
            remote(rows.at[c, slot(j, 0)], rows.at[c, slot(j, 1)], ys.at[j, 0, c], yr.at[j, 0, c], at_y(s)),
            remote(rows.at[c, slot(j, 0)], rows.at[c, slot(j, 2)], ys.at[j, 1, c], yr.at[j, 1, c], at_y(-s)),
            remote(rows.at[c, slot(j, 1)], rows.at[c, slot(j, 3)], ys.at[j, 2, c], yr.at[j, 2, c], at_y(s)),
        ]

    along_y = [[by_y(j, c) for c in (0, 1)] for j in range(E_WIN)]

    def spread(j, c):
        if j:
            by_z[j][c].wait_recv()
        start(along_y[j][c][:2])

    def relay(j, c):
        along_y[j][c][0].wait_recv()
        along_y[j][c][2].start()

    def landed(j):
        for c in (0, 1):
            along_y[j][c][1].wait_recv()
            along_y[j][c][2].wait_recv()

    def arrived(stage):
        for c in stage:
            c.wait_recv()

    def forward(lo, hi):
        pre[lo:hi] = jnp.zeros((hi - lo, 4 * SLICE), f32)
        dh[lo:hi] = jnp.zeros((hi - lo, 2 * SLICE), f32)

        @pl.loop(0, D // CHUNK)
        def _(n):
            cols = pl.ds(pl.multiple_of(n * CHUNK, 128), CHUNK)
            pre[lo:hi] += jnp.dot(rows[0, lo:hi, cols], w[cols, :], preferred_element_type=f32)
            dh[lo:hi] += lax.dot_general(rows[1, lo:hi, cols], down[:, cols], by_cols, preferred_element_type=f32)

    def pass_on(stage, n):
        if stage == 1:
            stage1[n].wait_recv()
            stage2[n].start()
        elif stage == 2:
            stage2[n].wait_recv()
            for group in stage3:
                group[n].start()
        else:
            for group in stage3:
                group[n].wait_recv()
            stage4[n].start()

    pl.semaphore_wait(barrier, len(peers))
    start(stage1)
    select(0)
    by_z[3][0].start()
    by_z[1][0].start()
    spread(0, 0)
    select(1)
    by_z[3][1].start()
    by_z[1][1].start()
    spread(0, 1)
    start(keep)
    pass_on(1, 0)
    relay(0, 0)
    pass_on(2, 0)
    pass_on(1, 1)
    relay(0, 1)
    by_z[2][0].start()
    by_z[2][1].start()
    spread(1, 0)
    spread(3, 0)
    pass_on(2, 1)
    pass_on(1, 2)
    spread(1, 1)
    spread(3, 1)
    pass_on(2, 2)
    relay(1, 0)
    relay(3, 0)
    pass_on(3, 0)
    relay(1, 1)
    relay(3, 1)
    spread(2, 0)
    pass_on(3, 1)
    spread(2, 1)
    relay(2, 0)
    pass_on(3, 2)
    relay(2, 1)
    for c in keep:
        c.wait()
    arrived(stage4)
    for j in ORDER[:3]:
        landed(j)
    forward(0, 3 * 64)
    landed(2)
    forward(3 * 64, N_ROWS)

    for h in (0, 1):
        a, b, c = 2 * h * SLICE, (2 * h + 1) * SLICE, (2 * h + 2) * SLICE
        gate, up, grad = pre[:, a:b], pre[:, b:c], dh[:, h * SLICE : (h + 1) * SLICE]
        sig = jax.nn.sigmoid(gate)
        silu = gate * sig
        hid[:, h * SLICE : (h + 1) * SLICE] = (silu * up).astype(bf)
        dcat[:, b:c] = (grad * silu).astype(bf)
        dcat[:, a:b] = (grad * up * sig * (1.0 + gate * (1.0 - sig))).astype(bf)

    near = {off: lax.rem(x + off, NX) for off in range(NX)}
    NEAR = (2, 1, 3, 0)
    LOW = ROWS // 2

    to_core = [remote(dw.at[k, :, :, 1 - core], theirs.at[k], cs.at[k], cr.at[k], sibling) for k in range(3)]
    first_pair = remote(dw.at[0, :, 1 - zl, core], from_pair, gs.at[0], gr.at[0], pair)

    def piece(k, off, t):
        n = near[off]
        return dw.at[k, n, t, core] if k else dw.at[0, n, zl, core, LOW * t : LOW * (t + 1)]

    def in_a(k, t):
        return from_a.at[k, t] if k else from_a.at[0, t, 0:LOW]

    def in_b(k, side, t):
        return from_b.at[k, side, t] if k else from_b.at[0, side, t, 0:LOW]

    by_a = [
        [
            remote(piece(k, 2, 0), in_a(k, 0), as_.at[k, 0], ar.at[k, 0], at_x(1)),
            remote(piece(k, 2, 1), in_a(k, 1), as_.at[k, 1], ar.at[k, 1], at_x(-1)),
        ]
        for k in range(3)
    ]
    by_b = [
        [
            remote(piece(k, 1, 1), in_b(k, 0, 1), bs.at[k, 0], br.at[k, 0], at_x(1)),
            remote(piece(k, 3, 0), in_b(k, 1, 0), bs.at[k, 1], br.at[k, 1], at_x(-1)),
            remote(piece(k, 1, 0), in_b(k, 0, 0), bs.at[k, 2], br.at[k, 2], at_x(1)),
            remote(piece(k, 3, 1), in_b(k, 1, 1), bs.at[k, 3], br.at[k, 3], at_x(-1)),
        ]
        for k in range(3)
    ]
    to_pair = remote(s2.at[0, 1 - zl], from_z, gs.at[4], gr.at[4], pair)
    to_y = remote(s3, from_y, fs.at[0], fr.at[0], at_y(4))
    spread_down = [
        remote(s2d.at[1 - zl, 1], from_d.at[2], fs.at[3], fr.at[3], diagonal),
        remote(s2d.at[zl, 1], from_d.at[1], fs.at[2], fr.at[2], at_y(4)),
        remote(s2d.at[1 - zl, 0], from_d.at[0], fs.at[1], fr.at[1], pair),
    ]

    def weight_grad(k):
        for off in NEAR:
            n = near[off]
            cols = pl.ds(pl.multiple_of(n * CHUNK, 128), CHUNK)
            right = hid[...] if k == 2 else dcat[:, 2 * SLICE * k : 2 * SLICE * (k + 1)]
            full = lax.dot_general(rows[k // 2, :, cols], right, by_rows, preferred_element_type=f32)
            dw[k, n] = full.astype(bf).reshape(2, 2, ROWS, 2 * SLICE)
        to_core[k].start()

    def leave_x(k, off):
        if off == 2:
            start(by_a[k])
        elif off and k == 0:
            by_b[k][off // 2].start()

    def rest(k):
        start(by_b[k][:2])

    def over_cores(k):
        to_core[k].wait_recv()
        for off in NEAR:
            n = near[off]
            for t in (0, 1):
                dw[k, n, t, core] = (dw[k, n, t, core].astype(f32) + theirs[k, n, t].astype(f32)).astype(bf)
            if k:
                leave_x(k, off)
        if k == 0:
            first_pair.start()

    def over_pair_first():
        first_pair.wait_recv()
        for off in NEAR:
            n = near[off]
            dw[0, n, zl, core] = (dw[0, n, zl, core].astype(f32) + from_pair[n].astype(f32)).astype(bf)
            leave_x(0, off)

    def augment(k):
        for t, off in ((0, 1), (1, 3)):
            by_a[k][t].wait_recv()
            spot = piece(k, off, t)
            spot[...] = (spot[...].astype(f32) + in_a(k, t)[...].astype(f32)).astype(bf)
            by_b[k][2 + t].start()

    def x_total(k, t):
        return piece(k, 0, t)[...].astype(f32) + in_b(k, 0, t)[...].astype(f32) + in_b(k, 1, t)[...].astype(f32)

    def over_x(k):
        for c in by_b[k]:
            c.wait_recv()
        if k == 1:
            s2[0, 1 - zl] = x_total(1, 1 - zl).astype(bf)
            to_pair.start()
            s2[0, zl] = x_total(1, zl).astype(bf)
        elif k == 2:
            for t in (1 - zl, zl):
                total = x_total(2, t).astype(bf)
                s2d[t, 0] = total[:, :SLICE]
                s2d[t, 1] = total[:, SLICE:]
            start(spread_down)
        else:
            for t in (0, 1):
                total = x_total(0, t) * scale
                out_gate[LOW * t : LOW * (t + 1)] = total[:, :SLICE]
                out_up[LOW * t : LOW * (t + 1)] = total[:, SLICE:]

    def over_pair():
        to_pair.wait_recv()
        s3[...] = (s2[0, zl].astype(f32) + from_z[...].astype(f32)).astype(bf)
        to_y.start()

    def finish():
        to_y.wait_recv()
        out_gate[...] += from_y[:, :SLICE].astype(f32) * scale
        out_up[...] += from_y[:, SLICE:].astype(f32) * scale
        arrived(spread_down)
        total = s2d[zl, 0].astype(f32)
        for n in range(3):
            total += from_d[n].astype(f32)
        out_down[...] = total * scale

    def backward(j):
        s = LEAN[j]
        return [
            remote(px.at[slot(j, 3)], mid.at[j], ps.at[j, 0], pr.at[j, 0], at_y(-s)),
            remote(px.at[slot(j, 2)], parts.at[j, 1], ps.at[j, 1], pr.at[j, 1], at_y(s)),
            remote(px.at[slot(j, 1)], parts.at[j, 0], ps.at[j, 2], pr.at[j, 2], at_y(-s)),
        ]

    back = [backward(j) for j in range(E_WIN)]
    home = {j: remote(sums.at[j], ret.at[z], hs.at[j - 1], hr.at[j - 1], at_z(j)) for j in (1, 2, 3)}
    landing = {j: remote(sums.at[j], ret.at[lax.rem(z + 4 - j, E_WIN)], hs.at[j - 1], hr.at[j - 1], at_z(j)) for j in (1, 2, 3)}

    def input_grad():
        @pl.loop(0, D // CHUNK)
        def _(n):
            cols = pl.ds(pl.multiple_of(n * CHUNK, 128), CHUNK)
            px[:, cols] = lax.dot_general(dcat[...], w[cols, :], by_cols, preferred_element_type=f32).astype(bf)

    def leave(j):
        start(back[j][:2])

    def meet(j):
        back[j][0].wait_recv()
        spot = slot(j, 1)
        px[spot] = (px[spot].astype(f32) + mid[j].astype(f32)).astype(bf)
        back[j][2].start()

    def gather(j):
        arrived(back[j][1:])
        total = px[slot(j, 0)].astype(f32) + parts[j, 0].astype(f32) + parts[j, 1].astype(f32)
        if j:
            sums[j] = total.astype(bf)
            home[j].start()
        else:
            ret[z] = total.astype(bf)

    weight_grad(1)
    weight_grad(0)
    input_grad()
    leave(2)
    over_cores(1)
    rest(1)
    leave(1)
    over_cores(0)
    leave(3)
    weight_grad(2)
    leave(0)
    augment(1)
    meet(2)
    over_cores(2)
    rest(2)
    meet(1)
    meet(3)
    augment(2)
    meet(0)
    over_x(1)
    gather(2)
    over_pair()
    over_pair_first()
    gather(1)
    over_x(2)
    augment(0)
    gather(3)
    gather(0)
    over_x(0)
    finish()

    for j in (1, 2, 3):
        landing[j].wait_recv()
    for b in (0, 1):
        mine = ret[0]
        for e in range(1, E_WIN):
            mine = jnp.where(assign[b] == e, ret[e], mine)
        grad_in[b * BLK : (b + 1) * BLK] = mine

    groups = list(by_z.values()) + [g for both in along_y for g in both] + stage3 + [stage1, stage2, stage4]
    groups += back + by_a + by_b + [[to_pair, to_y, first_pair], to_core, spread_down, list(home.values())]
    for group in groups:
        for c in group:
            c.wait_send()


def layer(assign, tokens, cotangent, wg, wu, wd, scale):
    f32, bf = jnp.float32, jnp.bfloat16
    dma = pltpu.SemaphoreType.DMA
    anywhere = pl.BlockSpec(memory_space=pl.ANY)
    vmem = pl.BlockSpec(memory_space=pltpu.VMEM)
    return pl.pallas_call(
        functools.partial(layer_kernel, scale),
        out_shape=(
            jax.ShapeDtypeStruct((2 * BLK, D), bf),
            jax.ShapeDtypeStruct((ROWS, SLICE), f32),
            jax.ShapeDtypeStruct((ROWS, SLICE), f32),
            jax.ShapeDtypeStruct((ROWS, SLICE), f32),
        ),
        in_specs=[pl.BlockSpec(memory_space=pltpu.SMEM)] + [anywhere] * 5,
        out_specs=(vmem, vmem, vmem, vmem),
        scratch_shapes=[
            pltpu.VMEM((2, 2 * BLK, D), bf),
            pltpu.VMEM((2, E_WIN, BLK, D), bf),
            pltpu.VMEM((2, N_ROWS, D), bf),
            pltpu.VMEM((D, 4 * SLICE), bf),
            pltpu.VMEM((2 * SLICE, D), bf),
            pltpu.VMEM((N_ROWS, 4 * SLICE), f32),
            pltpu.VMEM((N_ROWS, 2 * SLICE), f32),
            pltpu.VMEM((N_ROWS, 4 * SLICE), bf),
            pltpu.VMEM((N_ROWS, 2 * SLICE), bf),
            pltpu.VMEM((N_ROWS, D), bf),
            pltpu.VMEM((3, NX, 2, 2, ROWS, 2 * SLICE), bf),
            pltpu.VMEM((3, NX, 2, ROWS, 2 * SLICE), bf),
            pltpu.VMEM((NX, ROWS, 2 * SLICE), bf),
            pltpu.VMEM((3, 2, ROWS, 2 * SLICE), bf),
            pltpu.VMEM((3, 2, 2, ROWS, 2 * SLICE), bf),
            pltpu.VMEM((1, 2, ROWS, 2 * SLICE), bf),
            pltpu.VMEM((ROWS, 2 * SLICE), bf),
            pltpu.VMEM((ROWS, 2 * SLICE), bf),
            pltpu.VMEM((ROWS, 2 * SLICE), bf),
            pltpu.VMEM((2, 2, ROWS, SLICE), bf),
            pltpu.VMEM((3, ROWS, SLICE), bf),
            pltpu.VMEM((E_WIN, BLK, D), bf),
            pltpu.VMEM((E_WIN, 2, BLK, D), bf),
            pltpu.VMEM((E_WIN, BLK, D), bf),
            pltpu.VMEM((E_WIN, BLK, D), bf),
            dma((5,)),
            dma((3, 2)), dma((3, 2)),
            dma((4, 3, 2)), dma((4, 3, 2)),
            dma((18,)), dma((18,)),
            dma((4, 3)), dma((4, 3)),
            dma((3,)), dma((3,)),
            dma((3,)), dma((3,)),
            dma((3, 2)), dma((3, 2)),
            dma((3, 4)), dma((3, 4)),
            dma((5,)), dma((5,)),
            dma((4,)), dma((4,)),
        ],
        compiler_params=pltpu.CompilerParams(collective_id=0, has_side_effects=True, vmem_limit_bytes=56 * 2**20),
        cost_estimate=pl.CostEstimate(flops=16 * N_ROWS * D * 2 * SLICE, bytes_accessed=2**24, transcendentals=0),
        name="layer",
    )(assign, tokens, cotangent, wg, wu, wd)


def hand_over_kernel(*refs):
    for n in range(4):
        refs[4 + n][...] = refs[n][...]


def hand_over(*arrays):
    vmem = pl.BlockSpec(memory_space=pltpu.VMEM)
    return pl.pallas_call(
        hand_over_kernel,
        out_shape=tuple(jax.ShapeDtypeStruct(a.shape, a.dtype) for a in arrays),
        in_specs=[vmem] * 4,
        out_specs=[vmem] * 4,
        name="hand_over",
    )(*arrays)


def shards(tokens, cotangent, assign, w_gate, w_up, w_down):
    scale = 1.0 / math.sqrt(lax.axis_size("expert") * lax.axis_size("replica") * BLK // 2)
    grad_in, gate, up, down = hand_over(*layer(assign, tokens, cotangent, w_gate, w_up, w_down, scale))
    return grad_in, gate, up, jnp.transpose(down)


def solution(mesh):
    placed = (
        P(("expert", "replica"), None),
        P(("expert", "replica"), None),
        P(("expert", "replica")),
        P(None, "expert"),
        P(None, "expert"),
        P("expert", None),
    )
    return jax.shard_map(
        shards,
        mesh=mesh,
        in_specs=placed,
        out_specs=(
            P(("expert", "replica"), None),
            P("replica", "expert"),
            P("replica", "expert"),
            P("expert", "replica"),
        ),
        check_vma=False,
    )
```

```python
import functools
import math

import jax
import jax.numpy as jnp
from jax import lax
from jax.experimental import pallas as pl
from jax.experimental.pallas import tpu as pltpu
from jax.sharding import PartitionSpec as P

E_WIN = 4
NY = 8
NX = 4
BLK = 16
D = 3584
SLICE = 128
ROWS = 224
CHUNK = 896
N_ROWS = 256
MESH = pl.DeviceIdType.MESH
LEAN = (1, -1, -1, 1)
ORDER = (0, 1, 3, 2)


def place():
    ex = lax.axis_index("expert")
    rp = lax.axis_index("replica")
    z, y = lax.div(ex, NY), lax.rem(ex, NY)
    q, core = lax.div(rp, 2), lax.rem(rp, 2)
    x, zl = lax.div(q, 2), lax.rem(q, 2)

    def at_z(i):
        return (lax.rem(z + i, E_WIN) * NY + y, rp)

    def at_y(d):
        return (z * NY + lax.rem(y + NY + d, NY), rp)

    def at_x(i):
        return (ex, lax.rem(x + NX + i, NX) * 4 + zl * 2 + core)

    pair = (ex, x * 4 + (1 - zl) * 2 + core)
    sibling = (ex, q * 2 + 1 - core)
    diagonal = (at_y(4)[0], pair[1])
    return z, x, zl, q, core, at_z, at_y, at_x, pair, sibling, diagonal


def remote(src, dst, send_sem, recv_sem, peer):
    return pltpu.make_async_remote_copy(
        src_ref=src, dst_ref=dst, send_sem=send_sem, recv_sem=recv_sem, device_id=peer, device_id_type=MESH
    )


def start(copies):
    for c in copies:
        c.start()


def slot(j, o):
    return pl.ds((ORDER.index(j) * 4 + o) * BLK, BLK)


def layer_kernel(scale, assign, tokens, cotangent, wg, wu, wd, grad_in, out_gate, out_up, out_down,
                 own, send, rows, w, down, pre, dh, dcat, hid, px, dw, theirs, from_pair, from_a, from_b, s2, from_z, s3, from_y,
                 s2d, from_d, mid, parts, sums, ret,
                 ls, zs, zr, ys, yr, ws, wr, ps, pr, hs, hr, cs, cr, as_, ar, bs, br, gs, gr, fs, fr):
    f32, bf = jnp.float32, jnp.bfloat16
    by_cols = (((1,), (1,)), ((), ()))
    by_rows = (((0,), (0,)), ((), ()))
    z, x, zl, q, core, at_z, at_y, at_x, pair, sibling, diagonal = place()

    peers = [at_z(i) for i in (1, 2, 3)] + [at_y(d) for d in (1, -1, 4)] + [at_x(i) for i in (1, 2, 3)] + [pair, sibling, diagonal]
    barrier = pltpu.get_barrier_semaphore()
    for peer in peers:
        pl.semaphore_signal(barrier, inc=1, device_id=peer, device_id_type=MESH)

    bring = [pltpu.make_async_copy(src, own.at[c], ls.at[3 + c]) for c, src in enumerate((tokens, cotangent))]
    start(bring)
    keep = [
        pltpu.make_async_copy(wg, w.at[:, 0:SLICE], ls.at[0]),
        pltpu.make_async_copy(wu, w.at[:, SLICE : 2 * SLICE], ls.at[1]),
        pltpu.make_async_copy(wd, down.at[0:SLICE], ls.at[2]),
    ]
    def select(c):
        bring[c].wait()
        first, second = own[c, 0:BLK], own[c, BLK : 2 * BLK]
        for e in range(E_WIN):
            other = jnp.where(assign[1] == e, second, jnp.zeros_like(second))
            send[c, e] = jnp.where(assign[0] == e, first, other)
        rows[c, slot(0, 0)] = send[c, z]

    half = pl.ds(pl.multiple_of(core * (D // 2), 128), D // 2)

    def weights(srcs, dsts, base, peer):
        return [remote(s, d, ws.at[base + n], wr.at[base + n], peer) for n, (s, d) in enumerate(zip(srcs, dsts))]

    def part(first, count):
        tall = pl.ds(pl.multiple_of(core * (D // 2) + first * ROWS, 32), count * ROWS)
        short = pl.ds(pl.multiple_of(SLICE + first * BLK, 16), count * BLK)
        return [w.at[tall, 2 * SLICE : 3 * SLICE], w.at[tall, 3 * SLICE : 4 * SLICE], down.at[short, half]]

    tall = pl.ds(pl.multiple_of(core * (D // 2) + q * ROWS, 32), ROWS)
    short = pl.ds(pl.multiple_of(q * BLK, 16), BLK)
    one, two, every = part(q, 1), part(2 * x, 2), part(0, 8)
    stage1 = weights([wg.at[tall], wu.at[tall], wd.at[short, half]], one, 0, at_y(4))
    stage2 = weights(one, one, 3, pair)
    stage3 = [weights(two, two, 6 + 3 * (i - 1), at_x(i)) for i in (1, 2, 3)]
    stage4 = weights(every, every, 15, sibling)

    by_z = {
        4 - i: [
            remote(send.at[c, lax.rem(z + i, E_WIN)], rows.at[c, slot(4 - i, 0)], zs.at[i - 1, c], zr.at[3 - i, c], at_z(i))
            for c in (0, 1)
        ]
        for i in (1, 2, 3)
    }

    def by_y(j, c):
        s = LEAN[j]
        return [
            remote(rows.at[c, slot(j, 0)], rows.at[c, slot(j, 1)], ys.at[j, 0, c], yr.at[j, 0, c], at_y(s)),
            remote(rows.at[c, slot(j, 0)], rows.at[c, slot(j, 2)], ys.at[j, 1, c], yr.at[j, 1, c], at_y(-s)),
            remote(rows.at[c, slot(j, 1)], rows.at[c, slot(j, 3)], ys.at[j, 2, c], yr.at[j, 2, c], at_y(s)),
        ]

    along_y = [[by_y(j, c) for c in (0, 1)] for j in range(E_WIN)]

    def spread(j, c):
        if j:
            by_z[j][c].wait_recv()
        start(along_y[j][c][:2])

    def relay(j, c):
        along_y[j][c][0].wait_recv()
        along_y[j][c][2].start()

    def landed(j):
        for c in (0, 1):
            along_y[j][c][1].wait_recv()
            along_y[j][c][2].wait_recv()

    def arrived(stage):
        for c in stage:
            c.wait_recv()

    def forward(lo, hi):
        pre[lo:hi] = jnp.zeros((hi - lo, 4 * SLICE), f32)
        dh[lo:hi] = jnp.zeros((hi - lo, 2 * SLICE), f32)

        @pl.loop(0, D // CHUNK)
        def _(n):
            cols = pl.ds(pl.multiple_of(n * CHUNK, 128), CHUNK)
            pre[lo:hi] += jnp.dot(rows[0, lo:hi, cols], w[cols, :], preferred_element_type=f32)
            dh[lo:hi] += lax.dot_general(rows[1, lo:hi, cols], down[:, cols], by_cols, preferred_element_type=f32)

    def pass_on(stage, n):
        if stage == 1:
            stage1[n].wait_recv()
            stage2[n].start()
        elif stage == 2:
            stage2[n].wait_recv()
            for group in stage3:
                group[n].start()
        else:
            for group in stage3:
                group[n].wait_recv()
            stage4[n].start()

    pl.semaphore_wait(barrier, len(peers))
    start(stage1)
    select(0)
    by_z[3][0].start()
    by_z[1][0].start()
    spread(0, 0)
    select(1)
    by_z[3][1].start()
    by_z[1][1].start()
    spread(0, 1)
    start(keep)
    pass_on(1, 0)
    relay(0, 0)
    pass_on(2, 0)
    pass_on(1, 1)
    relay(0, 1)
    by_z[2][0].start()
    by_z[2][1].start()
    spread(1, 0)
    spread(3, 0)
    pass_on(2, 1)
    pass_on(1, 2)
    spread(1, 1)
    spread(3, 1)
    pass_on(2, 2)
    relay(1, 0)
    relay(3, 0)
    pass_on(3, 0)
    relay(1, 1)
    relay(3, 1)
    spread(2, 0)
    pass_on(3, 1)
    spread(2, 1)
    relay(2, 0)
    pass_on(3, 2)
    relay(2, 1)
    for c in keep:
        c.wait()
    arrived(stage4)
    for j in ORDER[:3]:
        landed(j)
    forward(0, 3 * 64)
    landed(2)
    forward(3 * 64, N_ROWS)

    for h in (0, 1):
        a, b, c = 2 * h * SLICE, (2 * h + 1) * SLICE, (2 * h + 2) * SLICE
        gate, up, grad = pre[:, a:b], pre[:, b:c], dh[:, h * SLICE : (h + 1) * SLICE]
        sig = jax.nn.sigmoid(gate)
        silu = gate * sig
        hid[:, h * SLICE : (h + 1) * SLICE] = (silu * up).astype(bf)
        dcat[:, b:c] = (grad * silu).astype(bf)
        dcat[:, a:b] = (grad * up * sig * (1.0 + gate * (1.0 - sig))).astype(bf)

    near = {off: lax.rem(x + off, NX) for off in range(NX)}
    NEAR = (2, 1, 3, 0)
    LOW = ROWS // 2

    to_core = [remote(dw.at[k, :, :, 1 - core], theirs.at[k], cs.at[k], cr.at[k], sibling) for k in range(3)]
    first_pair = remote(dw.at[0, :, 1 - zl, core], from_pair, gs.at[0], gr.at[0], pair)

    def piece(k, off, t):
        n = near[off]
        return dw.at[k, n, t, core] if k else dw.at[0, n, zl, core, LOW * t : LOW * (t + 1)]

    def in_a(k, t):
        return from_a.at[k, t] if k else from_a.at[0, t, 0:LOW]

    def in_b(k, side, t):
        return from_b.at[k, side, t] if k else from_b.at[0, side, t, 0:LOW]

    by_a = [
        [
            remote(piece(k, 2, 0), in_a(k, 0), as_.at[k, 0], ar.at[k, 0], at_x(1)),
            remote(piece(k, 2, 1), in_a(k, 1), as_.at[k, 1], ar.at[k, 1], at_x(-1)),
        ]
        for k in range(3)
    ]
    by_b = [
        [
            remote(piece(k, 1, 1), in_b(k, 0, 1), bs.at[k, 0], br.at[k, 0], at_x(1)),
            remote(piece(k, 3, 0), in_b(k, 1, 0), bs.at[k, 1], br.at[k, 1], at_x(-1)),
            remote(piece(k, 1, 0), in_b(k, 0, 0), bs.at[k, 2], br.at[k, 2], at_x(1)),
            remote(piece(k, 3, 1), in_b(k, 1, 1), bs.at[k, 3], br.at[k, 3], at_x(-1)),
        ]
        for k in range(3)
    ]
    to_pair = remote(s2.at[0, 1 - zl], from_z, gs.at[4], gr.at[4], pair)
    to_y = remote(s3, from_y, fs.at[0], fr.at[0], at_y(4))
    spread_down = [
        remote(s2d.at[1 - zl, 1], from_d.at[2], fs.at[3], fr.at[3], diagonal),
        remote(s2d.at[zl, 1], from_d.at[1], fs.at[2], fr.at[2], at_y(4)),
        remote(s2d.at[1 - zl, 0], from_d.at[0], fs.at[1], fr.at[1], pair),
    ]

    def weight_grad(k):
        for off in NEAR:
            n = near[off]
            cols = pl.ds(pl.multiple_of(n * CHUNK, 128), CHUNK)
            right = hid[...] if k == 2 else dcat[:, 2 * SLICE * k : 2 * SLICE * (k + 1)]
            full = lax.dot_general(rows[k // 2, :, cols], right, by_rows, preferred_element_type=f32)
            dw[k, n] = full.astype(bf).reshape(2, 2, ROWS, 2 * SLICE)
        to_core[k].start()

    def leave_x(k, off):
        if off == 2:
            start(by_a[k])
        elif off and k == 0:
            by_b[k][off // 2].start()

    def rest(k):
        start(by_b[k][:2])

    def over_cores(k):
        to_core[k].wait_recv()
        for off in NEAR:
            n = near[off]
            for t in (0, 1):
                dw[k, n, t, core] = (dw[k, n, t, core].astype(f32) + theirs[k, n, t].astype(f32)).astype(bf)
            if k:
                leave_x(k, off)
        if k == 0:
            first_pair.start()

    def over_pair_first():
        first_pair.wait_recv()
        for off in NEAR:
            n = near[off]
            dw[0, n, zl, core] = (dw[0, n, zl, core].astype(f32) + from_pair[n].astype(f32)).astype(bf)
            leave_x(0, off)

    def augment(k):
        for t, off in ((0, 1), (1, 3)):
            by_a[k][t].wait_recv()
            spot = piece(k, off, t)
            spot[...] = (spot[...].astype(f32) + in_a(k, t)[...].astype(f32)).astype(bf)
            by_b[k][2 + t].start()

    def x_total(k, t):
        return piece(k, 0, t)[...].astype(f32) + in_b(k, 0, t)[...].astype(f32) + in_b(k, 1, t)[...].astype(f32)

    def over_x(k):
        for c in by_b[k]:
            c.wait_recv()
        if k == 1:
            s2[0, 1 - zl] = x_total(1, 1 - zl).astype(bf)
            to_pair.start()
            s2[0, zl] = x_total(1, zl).astype(bf)
        elif k == 2:
            for t in (1 - zl, zl):
                total = x_total(2, t).astype(bf)
                s2d[t, 0] = total[:, :SLICE]
                s2d[t, 1] = total[:, SLICE:]
            start(spread_down)
        else:
            for t in (0, 1):
                total = x_total(0, t) * scale
                out_gate[LOW * t : LOW * (t + 1)] = total[:, :SLICE]
                out_up[LOW * t : LOW * (t + 1)] = total[:, SLICE:]

    def over_pair():
        to_pair.wait_recv()
        s3[...] = (s2[0, zl].astype(f32) + from_z[...].astype(f32)).astype(bf)
        to_y.start()

    def finish():
        to_y.wait_recv()
        out_gate[...] += from_y[:, :SLICE].astype(f32) * scale
        out_up[...] += from_y[:, SLICE:].astype(f32) * scale
        arrived(spread_down)
        total = s2d[zl, 0].astype(f32)
        for n in range(3):
            total += from_d[n].astype(f32)
        out_down[...] = total * scale

    def backward(j):
        s = LEAN[j]
        return [
            remote(px.at[slot(j, 3)], mid.at[j], ps.at[j, 0], pr.at[j, 0], at_y(-s)),
            remote(px.at[slot(j, 2)], parts.at[j, 1], ps.at[j, 1], pr.at[j, 1], at_y(s)),
            remote(px.at[slot(j, 1)], parts.at[j, 0], ps.at[j, 2], pr.at[j, 2], at_y(-s)),
        ]

    back = [backward(j) for j in range(E_WIN)]
    home = {j: remote(sums.at[j], ret.at[z], hs.at[j - 1], hr.at[j - 1], at_z(j)) for j in (1, 2, 3)}
    landing = {j: remote(sums.at[j], ret.at[lax.rem(z + 4 - j, E_WIN)], hs.at[j - 1], hr.at[j - 1], at_z(j)) for j in (1, 2, 3)}

    def input_grad():
        @pl.loop(0, D // CHUNK)
        def _(n):
            cols = pl.ds(pl.multiple_of(n * CHUNK, 128), CHUNK)
            px[:, cols] = lax.dot_general(dcat[...], w[cols, :], by_cols, preferred_element_type=f32).astype(bf)

    def leave(j):
        start(back[j][:2])

    def meet(j):
        back[j][0].wait_recv()
        spot = slot(j, 1)
        px[spot] = (px[spot].astype(f32) + mid[j].astype(f32)).astype(bf)
        back[j][2].start()

    def gather(j):
        arrived(back[j][1:])
        total = px[slot(j, 0)].astype(f32) + parts[j, 0].astype(f32) + parts[j, 1].astype(f32)
        if j:
            sums[j] = total.astype(bf)
            home[j].start()
        else:
            ret[z] = total.astype(bf)

    weight_grad(1)
    weight_grad(0)
    weight_grad(2)
    input_grad()
    leave(2)
    over_cores(1)
    rest(1)
    leave(1)
    over_cores(0)
    leave(3)
    leave(0)
    augment(1)
    meet(2)
    over_cores(2)
    rest(2)
    meet(1)
    meet(3)
    augment(2)
    meet(0)
    over_x(1)
    gather(2)
    over_pair()
    over_pair_first()
    gather(1)
    over_x(2)
    augment(0)
    gather(3)
    gather(0)
    over_x(0)
    finish()

    for j in (1, 2, 3):
        landing[j].wait_recv()
    for b in (0, 1):
        mine = ret[0]
        for e in range(1, E_WIN):
            mine = jnp.where(assign[b] == e, ret[e], mine)
        grad_in[b * BLK : (b + 1) * BLK] = mine

    groups = list(by_z.values()) + [g for both in along_y for g in both] + stage3 + [stage1, stage2, stage4]
    groups += back + by_a + by_b + [[to_pair, to_y, first_pair], to_core, spread_down, list(home.values())]
    for group in groups:
        for c in group:
            c.wait_send()


def layer(assign, tokens, cotangent, wg, wu, wd, scale):
    f32, bf = jnp.float32, jnp.bfloat16
    dma = pltpu.SemaphoreType.DMA
    anywhere = pl.BlockSpec(memory_space=pl.ANY)
    vmem = pl.BlockSpec(memory_space=pltpu.VMEM)
    return pl.pallas_call(
        functools.partial(layer_kernel, scale),
        out_shape=(
            jax.ShapeDtypeStruct((2 * BLK, D), bf),
            jax.ShapeDtypeStruct((ROWS, SLICE), f32),
            jax.ShapeDtypeStruct((ROWS, SLICE), f32),
            jax.ShapeDtypeStruct((ROWS, SLICE), f32),
        ),
        in_specs=[pl.BlockSpec(memory_space=pltpu.SMEM)] + [anywhere] * 5,
        out_specs=(vmem, vmem, vmem, vmem),
        scratch_shapes=[
            pltpu.VMEM((2, 2 * BLK, D), bf),
            pltpu.VMEM((2, E_WIN, BLK, D), bf),
            pltpu.VMEM((2, N_ROWS, D), bf),
            pltpu.VMEM((D, 4 * SLICE), bf),
            pltpu.VMEM((2 * SLICE, D), bf),
            pltpu.VMEM((N_ROWS, 4 * SLICE), f32),
            pltpu.VMEM((N_ROWS, 2 * SLICE), f32),
            pltpu.VMEM((N_ROWS, 4 * SLICE), bf),
            pltpu.VMEM((N_ROWS, 2 * SLICE), bf),
            pltpu.VMEM((N_ROWS, D), bf),
            pltpu.VMEM((3, NX, 2, 2, ROWS, 2 * SLICE), bf),
            pltpu.VMEM((3, NX, 2, ROWS, 2 * SLICE), bf),
            pltpu.VMEM((NX, ROWS, 2 * SLICE), bf),
            pltpu.VMEM((3, 2, ROWS, 2 * SLICE), bf),
            pltpu.VMEM((3, 2, 2, ROWS, 2 * SLICE), bf),
            pltpu.VMEM((1, 2, ROWS, 2 * SLICE), bf),
            pltpu.VMEM((ROWS, 2 * SLICE), bf),
            pltpu.VMEM((ROWS, 2 * SLICE), bf),
            pltpu.VMEM((ROWS, 2 * SLICE), bf),
            pltpu.VMEM((2, 2, ROWS, SLICE), bf),
            pltpu.VMEM((3, ROWS, SLICE), bf),
            pltpu.VMEM((E_WIN, BLK, D), bf),
            pltpu.VMEM((E_WIN, 2, BLK, D), bf),
            pltpu.VMEM((E_WIN, BLK, D), bf),
            pltpu.VMEM((E_WIN, BLK, D), bf),
            dma((5,)),
            dma((3, 2)), dma((3, 2)),
            dma((4, 3, 2)), dma((4, 3, 2)),
            dma((18,)), dma((18,)),
            dma((4, 3)), dma((4, 3)),
            dma((3,)), dma((3,)),
            dma((3,)), dma((3,)),
            dma((3, 2)), dma((3, 2)),
            dma((3, 4)), dma((3, 4)),
            dma((5,)), dma((5,)),
            dma((4,)), dma((4,)),
        ],
        compiler_params=pltpu.CompilerParams(collective_id=0, has_side_effects=True, vmem_limit_bytes=56 * 2**20),
        cost_estimate=pl.CostEstimate(flops=16 * N_ROWS * D * 2 * SLICE, bytes_accessed=2**24, transcendentals=0),
        name="layer",
    )(assign, tokens, cotangent, wg, wu, wd)


def hand_over_kernel(*refs):
    for n in range(4):
        refs[4 + n][...] = refs[n][...]


def hand_over(*arrays):
    vmem = pl.BlockSpec(memory_space=pltpu.VMEM)
    return pl.pallas_call(
        hand_over_kernel,
        out_shape=tuple(jax.ShapeDtypeStruct(a.shape, a.dtype) for a in arrays),
        in_specs=[vmem] * 4,
        out_specs=[vmem] * 4,
        name="hand_over",
    )(*arrays)


def shards(tokens, cotangent, assign, w_gate, w_up, w_down):
    scale = 1.0 / math.sqrt(lax.axis_size("expert") * lax.axis_size("replica") * BLK // 2)
    grad_in, gate, up, down = hand_over(*layer(assign, tokens, cotangent, w_gate, w_up, w_down, scale))
    return grad_in, gate, up, jnp.transpose(down)


def solution(mesh):
    placed = (
        P(("expert", "replica"), None),
        P(("expert", "replica"), None),
        P(("expert", "replica")),
        P(None, "expert"),
        P(None, "expert"),
        P("expert", None),
    )
    return jax.shard_map(
        shards,
        mesh=mesh,
        in_specs=placed,
        out_specs=(
            P(("expert", "replica"), None),
            P("replica", "expert"),
            P("replica", "expert"),
            P("expert", "replica"),
        ),
        check_vma=False,
    )
```

```python
import functools
import math

import jax
import jax.numpy as jnp
from jax import lax
from jax.experimental import pallas as pl
from jax.experimental.pallas import tpu as pltpu
from jax.sharding import PartitionSpec as P

E_WIN = 4
NY = 8
NX = 4
BLK = 16
D = 3584
SLICE = 128
ROWS = 224
CHUNK = 896
N_ROWS = 256
MESH = pl.DeviceIdType.MESH
LEAN = (1, -1, -1, 1)
ORDER = (0, 1, 3, 2)


def place():
    ex = lax.axis_index("expert")
    rp = lax.axis_index("replica")
    z, y = lax.div(ex, NY), lax.rem(ex, NY)
    q, core = lax.div(rp, 2), lax.rem(rp, 2)
    x, zl = lax.div(q, 2), lax.rem(q, 2)

    def at_z(i):
        return (lax.rem(z + i, E_WIN) * NY + y, rp)

    def at_y(d):
        return (z * NY + lax.rem(y + NY + d, NY), rp)

    def at_x(i):
        return (ex, lax.rem(x + NX + i, NX) * 4 + zl * 2 + core)

    pair = (ex, x * 4 + (1 - zl) * 2 + core)
    sibling = (ex, q * 2 + 1 - core)
    diagonal = (at_y(4)[0], pair[1])
    return z, x, zl, q, core, at_z, at_y, at_x, pair, sibling, diagonal


def remote(src, dst, send_sem, recv_sem, peer):
    return pltpu.make_async_remote_copy(
        src_ref=src, dst_ref=dst, send_sem=send_sem, recv_sem=recv_sem, device_id=peer, device_id_type=MESH
    )


def start(copies):
    for c in copies:
        c.start()


def slot(j, o):
    return pl.ds((ORDER.index(j) * 4 + o) * BLK, BLK)


def layer_kernel(scale, assign, tokens, cotangent, wg, wu, wd, grad_in, out_gate, out_up, out_down,
                 own, send, rows, w, down, pre, dh, dcat, hid, px, dw, theirs, from_pair, from_a, from_b, s2, from_z, s3, from_y,
                 s2d, from_d, mid, parts, sums, ret,
                 ls, zs, zr, ys, yr, ws, wr, ps, pr, hs, hr, cs, cr, as_, ar, bs, br, gs, gr, fs, fr):
    f32, bf = jnp.float32, jnp.bfloat16
    by_cols = (((1,), (1,)), ((), ()))
    by_rows = (((0,), (0,)), ((), ()))
    z, x, zl, q, core, at_z, at_y, at_x, pair, sibling, diagonal = place()

    peers = [at_z(i) for i in (1, 2, 3)] + [at_y(d) for d in (1, -1, 4)] + [at_x(i) for i in (1, 2, 3)] + [pair, sibling, diagonal]
    barrier = pltpu.get_barrier_semaphore()
    for peer in peers:
        pl.semaphore_signal(barrier, inc=1, device_id=peer, device_id_type=MESH)

    bring = [pltpu.make_async_copy(src, own.at[c], ls.at[3 + c]) for c, src in enumerate((tokens, cotangent))]
    start(bring)
    keep = [
        pltpu.make_async_copy(wg, w.at[:, 0:SLICE], ls.at[0]),
        pltpu.make_async_copy(wu, w.at[:, SLICE : 2 * SLICE], ls.at[1]),
        pltpu.make_async_copy(wd, down.at[0:SLICE], ls.at[2]),
    ]
    def select(c):
        bring[c].wait()
        first, second = own[c, 0:BLK], own[c, BLK : 2 * BLK]
        for e in range(E_WIN):
            other = jnp.where(assign[1] == e, second, jnp.zeros_like(second))
            send[c, e] = jnp.where(assign[0] == e, first, other)
        rows[c, slot(0, 0)] = send[c, z]

    half = pl.ds(pl.multiple_of(core * (D // 2), 128), D // 2)

    def weights(srcs, dsts, base, peer):
        return [remote(s, d, ws.at[base + n], wr.at[base + n], peer) for n, (s, d) in enumerate(zip(srcs, dsts))]

    def part(first, count):
        tall = pl.ds(pl.multiple_of(core * (D // 2) + first * ROWS, 32), count * ROWS)
        short = pl.ds(pl.multiple_of(SLICE + first * BLK, 16), count * BLK)
        return [w.at[tall, 2 * SLICE : 3 * SLICE], w.at[tall, 3 * SLICE : 4 * SLICE], down.at[short, half]]

    tall = pl.ds(pl.multiple_of(core * (D // 2) + q * ROWS, 32), ROWS)
    short = pl.ds(pl.multiple_of(q * BLK, 16), BLK)
    one, two, every = part(q, 1), part(2 * x, 2), part(0, 8)
    stage1 = weights([wg.at[tall], wu.at[tall], wd.at[short, half]], one, 0, at_y(4))
    stage2 = weights(one, one, 3, pair)
    stage3 = [weights(two, two, 6 + 3 * (i - 1), at_x(i)) for i in (1, 2, 3)]
    stage4 = weights(every, every, 15, sibling)

    by_z = {
        4 - i: [
            remote(send.at[c, lax.rem(z + i, E_WIN)], rows.at[c, slot(4 - i, 0)], zs.at[i - 1, c], zr.at[3 - i, c], at_z(i))
            for c in (0, 1)
        ]
        for i in (1, 2, 3)
    }

    def by_y(j, c):
        s = LEAN[j]
        return [
            remote(rows.at[c, slot(j, 0)], rows.at[c, slot(j, 1)], ys.at[j, 0, c], yr.at[j, 0, c], at_y(s)),
            remote(rows.at[c, slot(j, 0)], rows.at[c, slot(j, 2)], ys.at[j, 1, c], yr.at[j, 1, c], at_y(-s)),
            remote(rows.at[c, slot(j, 1)], rows.at[c, slot(j, 3)], ys.at[j, 2, c], yr.at[j, 2, c], at_y(s)),
        ]

    along_y = [[by_y(j, c) for c in (0, 1)] for j in range(E_WIN)]

    def spread(j, c):
        if j:
            by_z[j][c].wait_recv()
        start(along_y[j][c][:2])

    def relay(j, c):
        along_y[j][c][0].wait_recv()
        along_y[j][c][2].start()

    def landed(j):
        for c in (0, 1):
            along_y[j][c][1].wait_recv()
            along_y[j][c][2].wait_recv()

    def arrived(stage):
        for c in stage:
            c.wait_recv()

    def forward(lo, hi):
        pre[lo:hi] = jnp.zeros((hi - lo, 4 * SLICE), f32)
        dh[lo:hi] = jnp.zeros((hi - lo, 2 * SLICE), f32)

        @pl.loop(0, D // CHUNK)
        def _(n):
            cols = pl.ds(pl.multiple_of(n * CHUNK, 128), CHUNK)
            pre[lo:hi] += jnp.dot(rows[0, lo:hi, cols], w[cols, :], preferred_element_type=f32)
            dh[lo:hi] += lax.dot_general(rows[1, lo:hi, cols], down[:, cols], by_cols, preferred_element_type=f32)

    def pass_on(stage, n):
        if stage == 1:
            stage1[n].wait_recv()
            stage2[n].start()
        elif stage == 2:
            stage2[n].wait_recv()
            for group in stage3:
                group[n].start()
        else:
            for group in stage3:
                group[n].wait_recv()
            stage4[n].start()

    pl.semaphore_wait(barrier, len(peers))
    start(stage1)
    select(0)
    by_z[3][0].start()
    by_z[1][0].start()
    spread(0, 0)
    select(1)
    by_z[3][1].start()
    by_z[1][1].start()
    spread(0, 1)
    start(keep)
    pass_on(1, 0)
    relay(0, 0)
    pass_on(2, 0)
    pass_on(1, 1)
    relay(0, 1)
    by_z[2][0].start()
    by_z[2][1].start()
    spread(1, 0)
    spread(3, 0)
    pass_on(2, 1)
    pass_on(1, 2)
    spread(1, 1)
    spread(3, 1)
    pass_on(2, 2)
    relay(1, 0)
    relay(3, 0)
    pass_on(3, 0)
    relay(1, 1)
    relay(3, 1)
    spread(2, 0)
    pass_on(3, 1)
    spread(2, 1)
    relay(2, 0)
    pass_on(3, 2)
    relay(2, 1)
    for c in keep:
        c.wait()
    arrived(stage4)
    for j in ORDER[:3]:
        landed(j)
    forward(0, 3 * 64)
    landed(2)
    forward(3 * 64, N_ROWS)

    for h in (0, 1):
        a, b, c = 2 * h * SLICE, (2 * h + 1) * SLICE, (2 * h + 2) * SLICE
        gate, up, grad = pre[:, a:b], pre[:, b:c], dh[:, h * SLICE : (h + 1) * SLICE]
        sig = jax.nn.sigmoid(gate)
        silu = gate * sig
        hid[:, h * SLICE : (h + 1) * SLICE] = (silu * up).astype(bf)
        dcat[:, b:c] = (grad * silu).astype(bf)
        dcat[:, a:b] = (grad * up * sig * (1.0 + gate * (1.0 - sig))).astype(bf)

    near = {off: lax.rem(x + off, NX) for off in range(NX)}
    NEAR = (2, 1, 3, 0)
    LOW = ROWS // 2

    to_core = [remote(dw.at[k, :, :, 1 - core], theirs.at[k], cs.at[k], cr.at[k], sibling) for k in range(3)]
    first_pair = remote(dw.at[0, :, 1 - zl, core], from_pair, gs.at[0], gr.at[0], pair)

    def piece(k, off, t):
        n = near[off]
        return dw.at[k, n, t, core] if k else dw.at[0, n, zl, core, LOW * t : LOW * (t + 1)]

    def in_a(k, t):
        return from_a.at[k, t] if k else from_a.at[0, t, 0:LOW]

    def in_b(k, side, t):
        return from_b.at[k, side, t] if k else from_b.at[0, side, t, 0:LOW]

    by_a = [
        [
            remote(piece(k, 2, 0), in_a(k, 0), as_.at[k, 0], ar.at[k, 0], at_x(1)),
            remote(piece(k, 2, 1), in_a(k, 1), as_.at[k, 1], ar.at[k, 1], at_x(-1)),
        ]
        for k in range(3)
    ]
    by_b = [
        [
            remote(piece(k, 1, 1), in_b(k, 0, 1), bs.at[k, 0], br.at[k, 0], at_x(1)),
            remote(piece(k, 3, 0), in_b(k, 1, 0), bs.at[k, 1], br.at[k, 1], at_x(-1)),
            remote(piece(k, 1, 0), in_b(k, 0, 0), bs.at[k, 2], br.at[k, 2], at_x(1)),
            remote(piece(k, 3, 1), in_b(k, 1, 1), bs.at[k, 3], br.at[k, 3], at_x(-1)),
        ]
        for k in range(3)
    ]
    to_pair = remote(s2.at[0, 1 - zl], from_z, gs.at[4], gr.at[4], pair)
    to_y = remote(s3, from_y, fs.at[0], fr.at[0], at_y(4))
    spread_down = [
        remote(s2d.at[1 - zl, 1], from_d.at[2], fs.at[3], fr.at[3], diagonal),
        remote(s2d.at[zl, 1], from_d.at[1], fs.at[2], fr.at[2], at_y(4)),
        remote(s2d.at[1 - zl, 0], from_d.at[0], fs.at[1], fr.at[1], pair),
    ]

    def weight_grad(k):
        for off in NEAR:
            n = near[off]
            cols = pl.ds(pl.multiple_of(n * CHUNK, 128), CHUNK)
            right = hid[...] if k == 2 else dcat[:, 2 * SLICE * k : 2 * SLICE * (k + 1)]
            full = lax.dot_general(rows[k // 2, :, cols], right, by_rows, preferred_element_type=f32)
            dw[k, n] = full.astype(bf).reshape(2, 2, ROWS, 2 * SLICE)
        to_core[k].start()

    def leave_x(k, off):
        if off == 2:
            start(by_a[k])
        elif off and k == 0:
            by_b[k][off // 2].start()

    def rest(k):
        start(by_b[k][:2])

    def over_cores(k):
        to_core[k].wait_recv()
        for off in NEAR:
            n = near[off]
            for t in (0, 1):
                dw[k, n, t, core] = (dw[k, n, t, core].astype(f32) + theirs[k, n, t].astype(f32)).astype(bf)
            if k:
                leave_x(k, off)
        if k == 0:
            first_pair.start()

    def over_pair_first():
        first_pair.wait_recv()
        for off in NEAR:
            n = near[off]
            dw[0, n, zl, core] = (dw[0, n, zl, core].astype(f32) + from_pair[n].astype(f32)).astype(bf)
            leave_x(0, off)

    def augment(k):
        for t, off in ((0, 1), (1, 3)):
            by_a[k][t].wait_recv()
            spot = piece(k, off, t)
            spot[...] = (spot[...].astype(f32) + in_a(k, t)[...].astype(f32)).astype(bf)
            by_b[k][2 + t].start()

    def x_total(k, t):
        return piece(k, 0, t)[...].astype(f32) + in_b(k, 0, t)[...].astype(f32) + in_b(k, 1, t)[...].astype(f32)

    def over_x(k):
        for c in by_b[k]:
            c.wait_recv()
        if k == 1:
            s2[0, 1 - zl] = x_total(1, 1 - zl).astype(bf)
            to_pair.start()
            s2[0, zl] = x_total(1, zl).astype(bf)
        elif k == 2:
            for t in (1 - zl, zl):
                total = x_total(2, t).astype(bf)
                s2d[t, 0] = total[:, :SLICE]
                s2d[t, 1] = total[:, SLICE:]
            start(spread_down)
        else:
            for t in (0, 1):
                total = x_total(0, t) * scale
                out_gate[LOW * t : LOW * (t + 1)] = total[:, :SLICE]
                out_up[LOW * t : LOW * (t + 1)] = total[:, SLICE:]

    def over_pair():
        to_pair.wait_recv()
        s3[...] = (s2[0, zl].astype(f32) + from_z[...].astype(f32)).astype(bf)
        to_y.start()

    def finish():
        to_y.wait_recv()
        out_gate[...] += from_y[:, :SLICE].astype(f32) * scale
        out_up[...] += from_y[:, SLICE:].astype(f32) * scale
        arrived(spread_down)
        total = s2d[zl, 0].astype(f32)
        for n in range(3):
            total += from_d[n].astype(f32)
        out_down[...] = total * scale

    def backward(j):
        s = LEAN[j]
        return [
            remote(px.at[slot(j, 3)], mid.at[j], ps.at[j, 0], pr.at[j, 0], at_y(-s)),
            remote(px.at[slot(j, 2)], parts.at[j, 1], ps.at[j, 1], pr.at[j, 1], at_y(s)),
            remote(px.at[slot(j, 1)], parts.at[j, 0], ps.at[j, 2], pr.at[j, 2], at_y(-s)),
        ]

    back = [backward(j) for j in range(E_WIN)]
    home = {j: remote(sums.at[j], ret.at[z], hs.at[j - 1], hr.at[j - 1], at_z(j)) for j in (1, 2, 3)}
    landing = {j: remote(sums.at[j], ret.at[lax.rem(z + 4 - j, E_WIN)], hs.at[j - 1], hr.at[j - 1], at_z(j)) for j in (1, 2, 3)}

    def input_grad():
        @pl.loop(0, D // CHUNK)
        def _(n):
            cols = pl.ds(pl.multiple_of(n * CHUNK, 128), CHUNK)
            px[:, cols] = lax.dot_general(dcat[...], w[cols, :], by_cols, preferred_element_type=f32).astype(bf)

    def leave(j):
        start(back[j][:2])

    def meet(j):
        back[j][0].wait_recv()
        spot = slot(j, 1)
        px[spot] = (px[spot].astype(f32) + mid[j].astype(f32)).astype(bf)
        back[j][2].start()

    def gather(j):
        arrived(back[j][1:])
        total = px[slot(j, 0)].astype(f32) + parts[j, 0].astype(f32) + parts[j, 1].astype(f32)
        if j:
            sums[j] = total.astype(bf)
            home[j].start()
        else:
            ret[z] = total.astype(bf)

    weight_grad(1)
    weight_grad(0)
    over_cores(1)
    rest(1)
    input_grad()
    leave(2)
    leave(1)
    over_cores(0)
    leave(3)
    weight_grad(2)
    leave(0)
    augment(1)
    meet(2)
    over_cores(2)
    rest(2)
    meet(1)
    meet(3)
    augment(2)
    meet(0)
    over_x(1)
    gather(2)
    over_pair()
    over_pair_first()
    gather(1)
    over_x(2)
    augment(0)
    gather(3)
    gather(0)
    over_x(0)
    finish()

    for j in (1, 2, 3):
        landing[j].wait_recv()
    for b in (0, 1):
        mine = ret[0]
        for e in range(1, E_WIN):
            mine = jnp.where(assign[b] == e, ret[e], mine)
        grad_in[b * BLK : (b + 1) * BLK] = mine

    groups = list(by_z.values()) + [g for both in along_y for g in both] + stage3 + [stage1, stage2, stage4]
    groups += back + by_a + by_b + [[to_pair, to_y, first_pair], to_core, spread_down, list(home.values())]
    for group in groups:
        for c in group:
            c.wait_send()


def layer(assign, tokens, cotangent, wg, wu, wd, scale):
    f32, bf = jnp.float32, jnp.bfloat16
    dma = pltpu.SemaphoreType.DMA
    anywhere = pl.BlockSpec(memory_space=pl.ANY)
    vmem = pl.BlockSpec(memory_space=pltpu.VMEM)
    return pl.pallas_call(
        functools.partial(layer_kernel, scale),
        out_shape=(
            jax.ShapeDtypeStruct((2 * BLK, D), bf),
            jax.ShapeDtypeStruct((ROWS, SLICE), f32),
            jax.ShapeDtypeStruct((ROWS, SLICE), f32),
            jax.ShapeDtypeStruct((ROWS, SLICE), f32),
        ),
        in_specs=[pl.BlockSpec(memory_space=pltpu.SMEM)] + [anywhere] * 5,
        out_specs=(vmem, vmem, vmem, vmem),
        scratch_shapes=[
            pltpu.VMEM((2, 2 * BLK, D), bf),
            pltpu.VMEM((2, E_WIN, BLK, D), bf),
            pltpu.VMEM((2, N_ROWS, D), bf),
            pltpu.VMEM((D, 4 * SLICE), bf),
            pltpu.VMEM((2 * SLICE, D), bf),
            pltpu.VMEM((N_ROWS, 4 * SLICE), f32),
            pltpu.VMEM((N_ROWS, 2 * SLICE), f32),
            pltpu.VMEM((N_ROWS, 4 * SLICE), bf),
            pltpu.VMEM((N_ROWS, 2 * SLICE), bf),
            pltpu.VMEM((N_ROWS, D), bf),
            pltpu.VMEM((3, NX, 2, 2, ROWS, 2 * SLICE), bf),
            pltpu.VMEM((3, NX, 2, ROWS, 2 * SLICE), bf),
            pltpu.VMEM((NX, ROWS, 2 * SLICE), bf),
            pltpu.VMEM((3, 2, ROWS, 2 * SLICE), bf),
            pltpu.VMEM((3, 2, 2, ROWS, 2 * SLICE), bf),
            pltpu.VMEM((1, 2, ROWS, 2 * SLICE), bf),
            pltpu.VMEM((ROWS, 2 * SLICE), bf),
            pltpu.VMEM((ROWS, 2 * SLICE), bf),
            pltpu.VMEM((ROWS, 2 * SLICE), bf),
            pltpu.VMEM((2, 2, ROWS, SLICE), bf),
            pltpu.VMEM((3, ROWS, SLICE), bf),
            pltpu.VMEM((E_WIN, BLK, D), bf),
            pltpu.VMEM((E_WIN, 2, BLK, D), bf),
            pltpu.VMEM((E_WIN, BLK, D), bf),
            pltpu.VMEM((E_WIN, BLK, D), bf),
            dma((5,)),
            dma((3, 2)), dma((3, 2)),
            dma((4, 3, 2)), dma((4, 3, 2)),
            dma((18,)), dma((18,)),
            dma((4, 3)), dma((4, 3)),
            dma((3,)), dma((3,)),
            dma((3,)), dma((3,)),
            dma((3, 2)), dma((3, 2)),
            dma((3, 4)), dma((3, 4)),
            dma((5,)), dma((5,)),
            dma((4,)), dma((4,)),
        ],
        compiler_params=pltpu.CompilerParams(collective_id=0, has_side_effects=True, vmem_limit_bytes=56 * 2**20),
        cost_estimate=pl.CostEstimate(flops=16 * N_ROWS * D * 2 * SLICE, bytes_accessed=2**24, transcendentals=0),
        name="layer",
    )(assign, tokens, cotangent, wg, wu, wd)


def hand_over_kernel(*refs):
    for n in range(4):
        refs[4 + n][...] = refs[n][...]


def hand_over(*arrays):
    vmem = pl.BlockSpec(memory_space=pltpu.VMEM)
    return pl.pallas_call(
        hand_over_kernel,
        out_shape=tuple(jax.ShapeDtypeStruct(a.shape, a.dtype) for a in arrays),
        in_specs=[vmem] * 4,
        out_specs=[vmem] * 4,
        name="hand_over",
    )(*arrays)


def shards(tokens, cotangent, assign, w_gate, w_up, w_down):
    scale = 1.0 / math.sqrt(lax.axis_size("expert") * lax.axis_size("replica") * BLK // 2)
    grad_in, gate, up, down = hand_over(*layer(assign, tokens, cotangent, w_gate, w_up, w_down, scale))
    return grad_in, gate, up, jnp.transpose(down)


def solution(mesh):
    placed = (
        P(("expert", "replica"), None),
        P(("expert", "replica"), None),
        P(("expert", "replica")),
        P(None, "expert"),
        P(None, "expert"),
        P("expert", None),
    )
    return jax.shard_map(
        shards,
        mesh=mesh,
        in_specs=placed,
        out_specs=(
            P(("expert", "replica"), None),
            P("replica", "expert"),
            P("replica", "expert"),
            P("expert", "replica"),
        ),
        check_vma=False,
    )
```
